256 devices in a mesh: replica: 16 (over z_hi, x), fsdp: 8 (over y, core), tensor: 2 (over z_lo).
Axes of the slice: x: 4, y: 4, z: 8 (z_hi: 4, z_lo: 2; z = z_hi * 2 + z_lo), core: 2. Of those that a mesh axis runs over, the one named last changes fastest.
Arguments:
- activations: bfloat16 [49152, 8192], P(('replica', 'fsdp'), 'tensor'), may hold values from -6 to 6
- key_weight: bfloat16 [16, 8192, 512], P('replica', 'fsdp', 'tensor'), may hold values from -0.0625 to 0.0625
- key_cotangent: bfloat16 [49152, 512], P(('replica', 'fsdp'), 'tensor'), may hold values from -6 to 6
- outer_mantissa: bfloat16 [16, 4, 8192, 512], P('replica', None, 'fsdp', 'tensor'), may hold values from -6 to 6
- outer_exponent: int32 [16, 4, 8192, 4], P('replica', None, 'fsdp', 'tensor'), may hold values from -8 to -6
- round_index: int32 [1], replicated, may hold values from 0 to 65535
- global_weight: float32 [4, 8192, 512], P(None, ('fsdp', 'replica'), 'tensor'), may hold values from -0.0625 to 0.0625
- outer_momentum: float32 [4, 8192, 512], P(None, ('fsdp', 'replica'), 'tensor'), may hold values from -0.06 to 0.06
Outputs:
- key_states: bfloat16 [49152, 512], P(('replica', 'fsdp'), 'tensor')
- input_grad: bfloat16 [49152, 8192], P(('replica', 'fsdp'), 'tensor')
- weight_grad: bfloat16 [16, 8192, 512], P('replica', 'fsdp', 'tensor')
- global_weight_out: float32 [4, 8192, 512], P(None, ('fsdp', 'replica'), 'tensor')
- momentum_out: float32 [4, 8192, 512], P(None, ('fsdp', 'replica'), 'tensor')
- fragment_weight: bfloat16 [8192, 512], P('fsdp', 'tensor')
The draws below stay inside these ranges and needn't reach their ends.
All inputs are finite; a program needn't handle non-finite values.
Results may differ from the reference program's by a relative error of at most 0.017.
Values may be sent and summed in bfloat16 or wider, within the bound.
A program may use at most 128 MiB of HBM per device.

```python
import jax
import jax.numpy as jnp
from jax import lax

D = 8192
KV = 512
BLOCK = 128
FRAGS = 4
TOK_DEV = 384
TOKENS = 49152
N_REPLICA = 16
N_FSDP = 8
N_TENSOR = 2


def touch_ends(result, stream_key, low, top_value):
    dims = result.shape
    place = [jax.random.randint(jax.random.fold_in(stream_key, axis), (), 0, dims[axis]) for axis in range(len(dims))]
    result = result.at[tuple(place)].set(low)
    longest = dims.index(max(dims))
    place[longest] = (place[longest] + 1) % dims[longest]
    return result.at[tuple(place)].set(top_value)


def spiked(result, key, source, target, parts, factor):
    owner, partner = [(jnp.arange(result.shape[axis_at]) // (result.shape[axis_at] // parts)).reshape([-1 if axis == axis_at else 1 for axis in range(result.ndim)]) for axis_at in (source, target)]
    chosen = jax.random.permutation(key, parts)[partner]
    strong = (owner == chosen) | (owner == (partner + parts // 2) % parts)
    return jnp.where(strong, factor * result, result)


def levels(key, shape, split, least, top_value):
    def one(dim, blocks):
        heights = jax.random.uniform(jax.random.fold_in(jax.random.fold_in(key, 6), dim), (blocks,), jnp.float32, least / len(split), top_value / len(split))
        return jnp.repeat(jnp.exp(heights), shape[dim] // blocks).reshape((-1,) + (1,) * (len(shape) - dim - 1))

    loudness = one(*split[0])
    for cut in split[1:]:
        loudness = loudness * one(*cut)
    return loudness


def centred(key, shape, spread, most, cuts=(), held_as=jnp.bfloat16):
    values = spread * jax.random.normal(key, shape, jnp.float32)
    if cuts:
        values = values * levels(key, shape, cuts, -0.22, 0.18)
    return jnp.clip(values, -most, most).astype(held_as)


def noise_with(own_key, dims, spread, limit, shards, heavy, dtype=jnp.bfloat16):
    array = spread * jax.random.normal(own_key, dims, jnp.float32)
    if shards:
        array = array * levels(own_key, dims, shards, -0.22, 0.18)
    return jnp.clip(spiked(array, jax.random.fold_in(own_key, 3), *heavy), -limit, limit).astype(dtype)


def setup_inputs(seed: int = 0) -> dict:
    key_list = jax.random.split(jax.random.key(seed), 9)
    return {
        "activations": centred(key_list[0], (TOKENS, D), 1.0, 6.0, ((0, 128), (1, 2))),
        "key_weight": centred(key_list[1], (N_REPLICA, D, KV), D ** -0.5, 0.0625, ((0, 16), (1, 8), (2, 2))),
        "key_cotangent": centred(key_list[2], (TOKENS, KV), 1.0, 6.0, ((0, 128), (1, 2))),
        "outer_mantissa": noise_with(key_list[3], (N_REPLICA, FRAGS, D, KV), 1.0, 6.0, ((0, 16), (2, 8), (3, 2)), (0, 2, 16, 2.0)),
        "outer_exponent": touch_ends(jax.random.randint(key_list[4], (N_REPLICA, FRAGS, D, KV // BLOCK), -8, -5), jax.random.fold_in(key_list[4], 1), -8, (-5) - 1).astype(jnp.int32),
        "round_index": jax.random.randint(key_list[5], (1,), 0, 65536).astype(jnp.int32),
        "global_weight": centred(key_list[6], (FRAGS, D, KV), D ** -0.5, 0.0625, ((1, 128), (2, 2)), jnp.float32),
        "outer_momentum": centred(key_list[7], (FRAGS, D, KV), 0.01, 0.06, ((1, 128), (2, 2)), jnp.float32),
    }


outer_rate = 0.7
outer_beta = 0.9


def one_group(inputs):
    acts_group, weight_group, cots_group = inputs
    key_block = jnp.dot(acts_group, weight_group, preferred_element_type=jnp.float32).astype(jnp.bfloat16)
    split_acts = acts_group.reshape(N_FSDP, TOK_DEV, D).astype(jnp.float32)
    split_cots = cots_group.reshape(N_FSDP, TOK_DEV, KV).astype(jnp.float32)
    partial_value = jnp.einsum("ftd,ftk->fdk", split_acts, split_cots).astype(jnp.bfloat16)
    partial_value = lax.optimization_barrier(partial_value).astype(jnp.float32)
    grad_block = jnp.sum(partial_value, axis=0).astype(jnp.bfloat16)
    halves = KV // N_TENSOR
    cot_halves = cots_group.reshape(-1, N_TENSOR, halves).astype(jnp.float32)
    weight_halves = weight_group.reshape(D, N_TENSOR, halves).astype(jnp.float32)
    input_parts = jnp.einsum("mtk,dtk->tmd", cot_halves, weight_halves).astype(jnp.bfloat16)
    input_parts = lax.optimization_barrier(input_parts).astype(jnp.float32)
    input_block = jnp.sum(input_parts, axis=0).astype(jnp.bfloat16)
    return key_block, input_block, grad_block


def reference(activations, key_weight, key_cotangent, outer_mantissa, outer_exponent, round_index, global_weight, outer_momentum):
    group_rows = TOK_DEV * N_FSDP
    acts = activations.reshape(N_REPLICA, group_rows, D)
    cots = key_cotangent.reshape(N_REPLICA, group_rows, KV)
    key_parts, input_parts, weight_grad = lax.map(one_group, (acts, key_weight, cots))
    key_states = key_parts.reshape(-1, KV)
    input_grad = input_parts.reshape(-1, D)
    fragment = jnp.remainder(round_index[0], jnp.int32(FRAGS)).astype(jnp.int32)
    mantissa = lax.dynamic_index_in_dim(outer_mantissa, fragment, 1, False).astype(jnp.float32)
    exponent = lax.dynamic_index_in_dim(outer_exponent, fragment, 1, False).astype(jnp.float32)
    scales = jnp.repeat(jnp.exp2(exponent), BLOCK, axis=2)
    delta = jnp.sum(mantissa * scales, axis=0) / N_REPLICA
    old_moment = lax.dynamic_index_in_dim(outer_momentum, fragment, 0, False)
    old_weight = lax.dynamic_index_in_dim(global_weight, fragment, 0, False)
    new_moment = outer_beta * old_moment + delta
    new_weight = old_weight - outer_rate * (delta + outer_beta * new_moment)
    momentum_out = lax.dynamic_update_index_in_dim(outer_momentum, new_moment, fragment, 0)
    global_weight_out = lax.dynamic_update_index_in_dim(global_weight, new_weight, fragment, 0)
    fragment_weight = new_weight.astype(jnp.bfloat16)
    return key_states, input_grad, weight_grad, global_weight_out, momentum_out, fragment_weight
```

```python
import functools

import jax
import jax.numpy as jnp
from jax import lax
from jax.experimental import pallas as pl
from jax.experimental.pallas import tpu as pltpu
from jax.sharding import PartitionSpec as P

MESH = pl.DeviceIdType.MESH
F32 = jnp.float32
BF16 = jnp.bfloat16

TOK = 384
ROWS = 1024
COLS = 256
HALF = 512
WIDTH = 4096
STATE = 64
FRAGS = 4
RATE = 0.7
BETA = 0.9
LOADS = ("cot", "weight", "acts", "mant", "expo", "gw", "mom")
STORES = ("key", "wg0", "wg1", "gw", "mom", "frag", "ig0", "ig1", "ig2", "ig3")


def tt_dot(a, b):
    return lax.dot_general(a, b, (((0,), (0,)), ((), ())), preferred_element_type=F32)


def nt_dot(a, b):
    return lax.dot_general(a, b, (((1,), (1,)), ((), ())), preferred_element_type=F32)


def kernel(
    acts_hbm, weight_hbm, cot_hbm, mant_hbm, expo_hbm, round_ref, gw_hbm, mom_hbm,
    key_out, ig_out, wg_out, gw_out, mom_out, frag_out,
    acts, cot, wbuf, gsend, grecv, gsum, rv, rh, zr, ig, key, key_send, key_recv, key_final, wg,
    mant, expo, contrib, xr, xsum, zrecv, frag, gw, mom,
    ld, st, wv_s, wv_r, wh_s, wh_r, rv_s, rv_r, rh_s, rh_r, bw_s, bw_r, bg_s, bg_r, z_s, z_r,
    xs_s, xs_r, zs_s, zs_r, za_s, za_r, xa_s, xa_r,
):
    r = lax.axis_index("replica")
    f = lax.axis_index("fsdp")
    t = lax.axis_index("tensor")
    zh, x = r // 4, lax.rem(r, 4)
    y, c = f // 2, lax.rem(f, 2)
    odd = lax.rem(y, 2)
    near = (y // 2) == t
    far = (y // 2) != t
    ja = jnp.where(near, odd, 1 - odd)
    jb = 1 - ja
    cols = (t, 1 - t)
    dev_h = (r, (y + 1 - 2 * odd) * 2 + c, t)
    dev_v = (r, (3 - y) * 2 + c, t)
    dev_z = (r, f, 1 - t)
    dev_s = (r, y * 2 + 1 - c, t)
    dev_x = [(zh * 4 + lax.rem(x + d, 4), f, t) for d in (1, 2, 3)]
    dev_zh = [(lax.rem(zh + d, 4) * 4 + x, f, t) for d in (1, 2, 3)]

    barrier = pltpu.get_barrier_semaphore()
    everyone = [dev_h, dev_v, dev_z, dev_s, *dev_x, *dev_zh]
    for device in everyone:
        pl.semaphore_signal(barrier, inc=1, device_id=device, device_id_type=MESH)

    def load(name, src, dst):
        return pltpu.make_async_copy(src, dst, ld.at[LOADS.index(name)])

    def store(name, src, dst):
        copy = pltpu.make_async_copy(src, dst, st.at[STORES.index(name)])
        copy.start()
        return copy

    def remote(src, dst, s, r_, i, device):
        return pltpu.make_async_remote_copy(
            src_ref=src, dst_ref=dst, send_sem=s.at[i], recv_sem=r_.at[i], device_id=device, device_id_type=MESH
        )

    load_cot = load("cot", cot_hbm, cot.at[t])
    load_weight = load("weight", weight_hbm, wbuf.at[ja, c, t])
    load_acts = load("acts", acts_hbm, acts)
    load_mant = load("mant", mant_hbm, mant)
    load_expo = load("expo", expo_hbm, expo)
    load_gw = load("gw", gw_hbm, gw)
    load_mom = load("mom", mom_hbm, mom)
    load_cot.start()

    @pl.when(near)
    def _():
        load_weight.start()

    for one in (load_acts, load_mant, load_expo, load_gw, load_mom):
        one.start()

    def piece(j, plane, k, q):
        return wbuf.at[j, plane, cols[k], pl.ds(q * HALF, HALF)]

    def w_v(i, j, k, q):
        return remote(piece(j, c, k, q), piece(j, c, k, q), wv_s, wv_r, i, dev_v)

    def w_h(i, j, k, q):
        return remote(piece(j, c, k, q), piece(j, c, k, q), wh_s, wh_r, i, dev_h)

    def w_sib(w, k, q):
        j = (ja, jb)[w]
        return remote(piece(j, c, k, q), piece(j, c, k, q), bw_s, bw_r, w * 4 + k * 2 + q, dev_s)

    def w_from_sib(w, k, q):
        j = (ja, jb)[w]
        return remote(piece(j, 1 - c, k, q), piece(j, 1 - c, k, q), bw_s, bw_r, w * 4 + k * 2 + q, dev_s)

    def w_from_z(q):
        return remote(piece(ja, c, 1, q), piece(ja, c, 1, q), z_s, z_r, 1 + q, dev_z)

    def w_to_z(q):
        return remote(
            weight_hbm.at[pl.ds(q * HALF, HALF)], wbuf.at[odd, c, t, pl.ds(q * HALF, HALF)], z_s, z_r, 1 + q, dev_z
        )

    near_v = [(ja, 0, 0), (ja, 0, 1), (ja, 1, 0), (ja, 1, 1), (jb, 0, 1)]
    far_v = [(jb, 0, 0)]
    near_h = [(ja, 0, 1), (ja, 1, 0), (ja, 1, 1)]
    near_h_in = [(jb, 0, 1), (jb, 1, 0), (jb, 1, 1)]
    far_h = [(ja, 0, 0), (ja, 1, 0), (ja, 1, 1)]
    far_h_in = [(jb, 0, 0), (jb, 1, 0), (jb, 1, 1)]

    def part(p, j):
        return gsum.at[p // 2, j, p % 2]

    def g_v(i, src):
        return remote(src, rv.at[i], rv_s, rv_r, i, dev_v)

    def g_h(i, src):
        return remote(src, rh.at[i], rh_s, rh_r, i, dev_h)

    def add_into(dst, src):
        dst[...] = (dst[...].astype(F32) + src[...].astype(F32)).astype(BF16)

    pl.semaphore_wait(barrier, len(everyone))

    load_cot.wait()
    send_cot = remote(cot.at[t], cot.at[t], z_s, z_r, 0, dev_z)
    send_cot.start()

    @pl.when(near)
    def _():
        load_weight.wait()
        w_v(0, *near_v[0]).start()
        w_h(0, *near_h[0]).start()
        w_sib(0, 0, 0).start()
        w_sib(0, 0, 1).start()

    @pl.when(far)
    def _():
        w_to_z(0).start()
        w_to_z(1).start()

    def grad_blocks(k, plane, done):
        def body(i, _):
            j, q = i // 2, lax.rem(i, 2)
            at = pl.multiple_of(j * 2 * ROWS + plane * ROWS + q * HALF, HALF)
            done(j, q, tt_dot(acts[:, pl.ds(at, HALF)], cot[cols[k]]))
            return 0

        lax.fori_loop(0, 4, body, 0)

    def grad_send(k):
        def keep(j, q, block):
            gsend[k, j, q] = block.astype(BF16)

        grad_blocks(k, 1 - c, keep)
        copy = remote(gsend.at[k], grecv.at[k], bg_s, bg_r, k, dev_s)
        copy.start()
        return copy

    def grad_sum(k):
        def keep(j, q, block):
            gsum[k, j, q] = (block + grecv[k, j, q].astype(F32)).astype(BF16)

        grad_blocks(k, c, keep)

    load_acts.wait()
    send_g0 = grad_send(0)

    load_mant.wait()
    load_expo.wait()
    fragment = lax.rem(round_ref[0], FRAGS)
    power = jnp.exp2(expo[fragment].astype(F32))
    power = jnp.transpose(jnp.concatenate([power] * 4, axis=0))
    for h in range(2):
        block = mant[fragment, :, h * 128 : (h + 1) * 128].astype(F32) * power[:, h : h + 1]
        contrib[:, :, :, h * 128 : (h + 1) * 128] = block.astype(BF16).reshape(4, 4, STATE, 128)
    x_sends = [
        remote(contrib.at[:, lax.rem(x + d, 4)], xr.at[d - 1], xs_s, xs_r, d - 1, dev_x[d - 1]) for d in (1, 2, 3)
    ]
    for copy in x_sends:
        copy.start()

    send_g0.wait_recv()
    grad_sum(0)

    @pl.when(near)
    def _():
        g_h(1, part(1, jb)).start()
        w_v(1, *near_v[1]).start()

    @pl.when(far)
    def _():
        g_v(0, part(0, jb)).start()
        g_v(1, part(0, ja)).start()
        g_h(0, part(1, jb)).start()

    remote(cot.at[1 - t], cot.at[1 - t], z_s, z_r, 0, dev_z).wait_recv()
    send_g1 = grad_send(1)
    send_g1.wait_recv()
    grad_sum(1)

    @pl.when(near)
    def _():
        g_v(0, part(3, jb)).start()
        w_from_z(0).wait_recv()
        w_h(1, *near_h[1]).start()
        w_v(2, *near_v[2]).start()
        w_sib(0, 1, 0).start()
        w_from_z(1).wait_recv()
        w_h(2, *near_h[2]).start()
        w_v(3, *near_v[3]).start()
        w_sib(0, 1, 1).start()
        w_h(0, *near_h_in[0]).wait_recv()
        w_v(4, *near_v[4]).start()
        w_sib(1, 0, 1).start()
        g_h(2, part(2, jb)).start()
        g_v(0, rv.at[0]).wait_recv()
        add_into(rv.at[0], part(0, jb))
        g_h(0, rv.at[0]).start()

    @pl.when(far)
    def _():
        w_v(0, *near_v[0]).wait_recv()
        w_h(0, *far_h[0]).start()
        w_sib(0, 0, 0).start()
        g_h(1, part(2, jb)).start()
        w_h(0, *far_h_in[0]).wait_recv()
        w_v(0, *far_v[0]).start()
        w_sib(1, 0, 0).start()
        g_v(0, rv.at[0]).wait_recv()
        add_into(rv.at[0], part(3, jb))
        g_h(2, rv.at[0]).start()
        g_h(1, rh.at[1]).wait_recv()
        add_into(rh.at[1], part(2, ja))
        g_v(3, rh.at[1]).start()

    for copy in x_sends:
        copy.wait_recv()
    for i in range(4):
        total = contrib[i, x].astype(F32)
        for d in range(3):
            total = total + xr[d, i].astype(F32)
        xsum[i] = total.astype(BF16)
    z_sends = [
        remote(xsum.at[lax.rem(zh + d, 4)], zrecv.at[d - 1], zs_s, zs_r, d - 1, dev_zh[d - 1]) for d in (1, 2, 3)
    ]
    for copy in z_sends:
        copy.start()

    @pl.when(near)
    def _():
        w_h(1, *near_h_in[1]).wait_recv()
        w_sib(1, 1, 0).start()
        w_v(0, *far_v[0]).wait_recv()
        w_sib(1, 0, 0).start()
        w_h(2, *near_h_in[2]).wait_recv()
        w_sib(1, 1, 1).start()

    @pl.when(far)
    def _():
        w_v(1, *near_v[1]).wait_recv()
        w_sib(0, 0, 1).start()
        w_v(2, *near_v[2]).wait_recv()
        w_h(1, *far_h[1]).start()
        w_sib(0, 1, 0).start()
        g_h(2, rh.at[2]).wait_recv()
        add_into(rh.at[2], part(3, ja))
        g_v(4, rh.at[2]).start()
        g_h(0, rh.at[0]).wait_recv()
        add_into(rh.at[0], part(1, ja))
        g_v(2, rh.at[0]).start()

    load_gw.wait()
    load_mom.wait()
    for copy in z_sends:
        copy.wait_recv()
    total = xsum[zh].astype(F32)
    for d in range(3):
        total = total + zrecv[d].astype(F32)
    delta = total * (1.0 / 16)
    new_moment = BETA * mom[fragment] + delta
    new_weight = gw[fragment] - RATE * (delta + BETA * new_moment)
    for i in range(FRAGS):
        chosen = fragment == i
        mom[i] = jnp.where(chosen, new_moment, mom[i])
        gw[i] = jnp.where(chosen, new_weight, gw[i])
    frag[zh, x] = new_weight.astype(BF16)
    stores = [store("gw", gw, gw_out), store("mom", mom, mom_out)]
    za_sends = [remote(frag.at[zh, x], frag.at[zh, x], za_s, za_r, d - 1, dev_zh[d - 1]) for d in (1, 2, 3)]
    for copy in za_sends:
        copy.start()

    @pl.when(far)
    def _():
        w_v(3, *near_v[3]).wait_recv()
        w_h(2, *far_h[2]).start()
        w_sib(0, 1, 1).start()

    for d in (1, 2, 3):
        there = frag.at[lax.rem(zh + 4 - d, 4), x]
        remote(there, there, za_s, za_r, d - 1, dev_zh[d - 1]).wait_recv()
    xa_sends = [remote(frag.at[:, x], frag.at[:, x], xa_s, xa_r, d - 1, dev_x[d - 1]) for d in (1, 2, 3)]
    for copy in xa_sends:
        copy.start()

    key[...] = jnp.zeros_like(key)

    def block(w, plane):
        j = (ja, jb)[w]
        at = j * 2 * ROWS + plane * ROWS
        wide = pl.ds(pl.multiple_of(at, ROWS), ROWS)
        for k in range(2):
            key[k] += jnp.dot(acts[:, wide], wbuf[j, plane, cols[k]], preferred_element_type=F32)

        def body(i, _):
            rows = pl.ds(pl.multiple_of(i * COLS, COLS), COLS)
            total = nt_dot(cot[0], wbuf[j, plane, 0, rows]) + nt_dot(cot[1], wbuf[j, plane, 1, rows])
            ig[:, pl.ds(pl.multiple_of(at + i * COLS, COLS), COLS)] = total.astype(BF16)
            return 0

        lax.fori_loop(0, ROWS // COLS, body, 0)
        i = ("ig0", "ig1", "ig2", "ig3")[w * 2 + (0 if plane is c else 1)]
        return store(i, ig.at[:, wide], ig_out.at[:, wide])

    stores.append(block(0, c))
    for k in range(2):
        for q in range(2):
            w_from_sib(0, k, q).wait_recv()
    other = 1 - c
    stores.append(block(0, other))

    @pl.when(near)
    def _():
        g_v(3, rv.at[3]).wait_recv()
        g_h(2, rh.at[2]).wait_recv()
        add_into(rv.at[3], rh.at[2])
        add_into(rv.at[3], part(2, ja))
        remote(rv.at[3], zr.at[0], z_s, z_r, 4, dev_z).start()

    @pl.when(far)
    def _():
        w_v(4, *near_v[4]).wait_recv()
        w_sib(1, 0, 1).start()
        w_h(1, *far_h_in[1]).wait_recv()
        w_sib(1, 1, 0).start()
        w_h(2, *far_h_in[2]).wait_recv()
        w_sib(1, 1, 1).start()

    stores.append(block(1, c))
    for k in range(2):
        for q in range(2):
            w_from_sib(1, k, q).wait_recv()
    stores.append(block(1, other))

    key_send[...] = key[1].astype(BF16)
    send_key = remote(key_send, key_recv, z_s, z_r, 3, dev_z)
    send_key.start()

    @pl.when(near)
    def _():
        g_v(4, rv.at[4]).wait_recv()
        add_into(rv.at[4], part(3, ja))
        remote(rv.at[4], zr.at[1], z_s, z_r, 5, dev_z).start()
        g_v(1, rv.at[1]).wait_recv()
        g_h(0, rh.at[0]).wait_recv()
        total = rv[1].astype(F32) + rh[0].astype(F32) + gsum[0, ja, 0].astype(F32)
        wg[0] = total.astype(BF16)
        g_v(2, rv.at[2]).wait_recv()
        g_h(1, rh.at[1]).wait_recv()
        total = rv[2].astype(F32) + rh[1].astype(F32) + gsum[0, ja, 1].astype(F32)
        wg[1] = total.astype(BF16)
        store("wg0", wg.at[0], wg_out.at[0])
        store("wg1", wg.at[1], wg_out.at[1])

    @pl.when(far)
    def _():
        for q in range(2):
            remote(zr.at[q], zr.at[q], z_s, z_r, 4 + q, dev_z).wait_recv()
            store(f"wg{q}", zr.at[q], wg_out.at[q])

    for d in (1, 2, 3):
        there = frag.at[:, lax.rem(x + 4 - d, 4)]
        remote(there, there, xa_s, xa_r, d - 1, dev_x[d - 1]).wait_recv()
    stores.append(store("frag", frag, frag_out))

    send_key.wait_recv()
    key_final[...] = (key[0] + key_recv[...].astype(F32)).astype(BF16)
    stores.append(store("key", key_final, key_out))

    for copy in (send_cot, send_key, send_g0, send_g1, *x_sends, *z_sends, *za_sends, *xa_sends):
        copy.wait_send()
    for w in range(2):
        for k in range(2):
            for q in range(2):
                w_sib(w, k, q).wait_send()
    for i in range(3):
        g_h(i, rh.at[i]).wait_send()

    @pl.when(near)
    def _():
        for i in range(5):
            w_v(i, *near_v[i]).wait_send()
        for i in range(3):
            w_h(i, *near_h[i]).wait_send()
        g_v(0, rv.at[0]).wait_send()
        for q in range(2):
            remote(rv.at[3 + q], zr.at[q], z_s, z_r, 4 + q, dev_z).wait_send()
        for q in range(2):
            pltpu.make_async_copy(wg.at[q], wg_out.at[q], st.at[STORES.index(f"wg{q}")]).wait()

    @pl.when(far)
    def _():
        w_v(0, *far_v[0]).wait_send()
        for i in range(3):
            w_h(i, *far_h[i]).wait_send()
        for i in range(5):
            g_v(i, rv.at[i]).wait_send()
        for q in range(2):
            w_to_z(q).wait_send()
        for q in range(2):
            pltpu.make_async_copy(zr.at[q], wg_out.at[q], st.at[STORES.index(f"wg{q}")]).wait()

    for copy in stores:
        copy.wait()


def local(
    activations, key_weight, key_cotangent, outer_mantissa, outer_exponent, round_index, global_weight, outer_momentum
):
    vmem = pltpu.VMEM
    dma = lambda n: pltpu.SemaphoreType.DMA((n,))
    exponent = jnp.transpose(outer_exponent[0], (0, 2, 1))
    anywhere = pl.BlockSpec(memory_space=pl.ANY)
    outs = pl.pallas_call(
        kernel,
        out_shape=(
            jax.ShapeDtypeStruct((TOK, COLS), BF16),
            jax.ShapeDtypeStruct((TOK, WIDTH), BF16),
            jax.ShapeDtypeStruct((2, HALF, COLS), BF16),
            jax.ShapeDtypeStruct((FRAGS, STATE, COLS), F32),
            jax.ShapeDtypeStruct((FRAGS, STATE, COLS), F32),
            jax.ShapeDtypeStruct((4, 4, STATE, COLS), BF16),
        ),
        in_specs=[anywhere] * 5 + [pl.BlockSpec(memory_space=pltpu.SMEM)] + [anywhere] * 2,
        out_specs=[anywhere] * 6,
        scratch_shapes=[
            vmem((TOK, WIDTH), BF16),
            vmem((2, TOK, COLS), BF16),
            vmem((2, 2, 2, ROWS, COLS), BF16),
            vmem((2, 2, 2, HALF, COLS), BF16),
            vmem((2, 2, 2, HALF, COLS), BF16),
            vmem((2, 2, 2, HALF, COLS), BF16),
            vmem((5, HALF, COLS), BF16),
            vmem((3, HALF, COLS), BF16),
            vmem((2, HALF, COLS), BF16),
            vmem((TOK, WIDTH), BF16),
            vmem((2, TOK, COLS), F32),
            vmem((TOK, COLS), BF16),
            vmem((TOK, COLS), BF16),
            vmem((TOK, COLS), BF16),
            vmem((2, HALF, COLS), BF16),
            vmem((FRAGS, ROWS, COLS), BF16),
            vmem((FRAGS, 2, ROWS), jnp.int32),
            vmem((4, 4, STATE, COLS), BF16),
            vmem((3, 4, STATE, COLS), BF16),
            vmem((4, STATE, COLS), BF16),
            vmem((3, STATE, COLS), BF16),
            vmem((4, 4, STATE, COLS), BF16),
            vmem((FRAGS, STATE, COLS), F32),
            vmem((FRAGS, STATE, COLS), F32),
            dma(len(LOADS)), dma(len(STORES)),
            dma(5), dma(5), dma(3), dma(3), dma(5), dma(5), dma(3), dma(3),
            dma(8), dma(8), dma(2), dma(2), dma(6), dma(6),
            dma(3), dma(3), dma(3), dma(3), dma(3), dma(3), dma(3), dma(3),
        ],
        compiler_params=pltpu.CompilerParams(
            collective_id=0, has_side_effects=True, vmem_limit_bytes=44 * 2**20
        ),
    )(
        activations, key_weight[0], key_cotangent, outer_mantissa[0], exponent, round_index, global_weight,
        outer_momentum,
    )
    key_states, input_grad, weight_grad, global_weight_out, momentum_out, fragment_weight = outs
    return (
        key_states,
        input_grad,
        weight_grad.reshape(1, ROWS, COLS),
        global_weight_out,
        momentum_out,
        fragment_weight.reshape(ROWS, COLS),
    )


def solution(mesh):
    placed = (
        P(("replica", "fsdp"), "tensor"),
        P("replica", "fsdp", "tensor"),
        P(("replica", "fsdp"), "tensor"),
        P("replica", None, "fsdp", "tensor"),
        P("replica", None, "fsdp", "tensor"),
        P(),
        P(None, ("fsdp", "replica"), "tensor"),
        P(None, ("fsdp", "replica"), "tensor"),
    )
    return jax.shard_map(
        local,
        mesh=mesh,
        in_specs=placed,
        out_specs=(
            P(("replica", "fsdp"), "tensor"),
            P(("replica", "fsdp"), "tensor"),
            P("replica", "fsdp", "tensor"),
            P(None, ("fsdp", "replica"), "tensor"),
            P(None, ("fsdp", "replica"), "tensor"),
            P("fsdp", "tensor"),
        ),
        check_vma=False,
    )
```

```python
import functools

import jax
import jax.numpy as jnp
from jax import lax
from jax.experimental import pallas as pl
from jax.experimental.pallas import tpu as pltpu
from jax.sharding import PartitionSpec as P

MESH = pl.DeviceIdType.MESH
F32 = jnp.float32
BF16 = jnp.bfloat16

TOK = 384
ROWS = 1024
COLS = 256
HALF = 512
WIDTH = 4096
STATE = 64
FRAGS = 4
RATE = 0.7
BETA = 0.9
LOADS = ("cot", "weight", "acts", "mant", "expo", "gw", "mom")


def tt_dot(a, b):
    return lax.dot_general(a, b, (((0,), (0,)), ((), ())), preferred_element_type=F32)


def nt_dot(a, b):
    return lax.dot_general(a, b, (((1,), (1,)), ((), ())), preferred_element_type=F32)


def kernel(
    acts_hbm, weight_hbm, cot_hbm, mant_hbm, expo_hbm, round_ref, gw_hbm, mom_hbm,
    key_out, ig_out, wg_out, gw_out, mom_out, frag_out,
    acts, cot, wbuf, gsend, grecv, gsum, rv, rh, zr, key, key_send, key_recv,
    mant, expo, contrib, xr, xsum, zrecv, frag, gw, mom,
    ld, wv_s, wv_r, wh_s, wh_r, rv_s, rv_r, rh_s, rh_r, bw_s, bw_r, bg_s, bg_r, z_s, z_r,
    xs_s, xs_r, zs_s, zs_r, za_s, za_r, xa_s, xa_r,
):
    r = lax.axis_index("replica")
    f = lax.axis_index("fsdp")
    t = lax.axis_index("tensor")
    zh, x = r // 4, lax.rem(r, 4)
    y, c = f // 2, lax.rem(f, 2)
    odd = lax.rem(y, 2)
    near = (y // 2) == t
    far = (y // 2) != t
    ja = jnp.where(near, odd, 1 - odd)
    jb = 1 - ja
    cols = (t, 1 - t)
    dev_h = (r, (y + 1 - 2 * odd) * 2 + c, t)
    dev_v = (r, (3 - y) * 2 + c, t)
    dev_z = (r, f, 1 - t)
    dev_s = (r, y * 2 + 1 - c, t)
    dev_x = [(zh * 4 + lax.rem(x + d, 4), f, t) for d in (1, 2, 3)]
    dev_zh = [(lax.rem(zh + d, 4) * 4 + x, f, t) for d in (1, 2, 3)]

    barrier = pltpu.get_barrier_semaphore()
    everyone = [dev_h, dev_v, dev_z, dev_s, *dev_x, *dev_zh]
    for device in everyone:
        pl.semaphore_signal(barrier, inc=1, device_id=device, device_id_type=MESH)

    def load(name, src, dst):
        return pltpu.make_async_copy(src, dst, ld.at[LOADS.index(name)])

    def remote(src, dst, s, r_, i, device):
        return pltpu.make_async_remote_copy(
            src_ref=src, dst_ref=dst, send_sem=s.at[i], recv_sem=r_.at[i], device_id=device, device_id_type=MESH
        )

    load_cot = load("cot", cot_hbm, cot.at[t])
    load_weight = load("weight", weight_hbm, wbuf.at[ja, c, t])
    load_acts = load("acts", acts_hbm, acts)
    load_mant = load("mant", mant_hbm, mant)
    load_expo = load("expo", expo_hbm, expo)
    load_gw = load("gw", gw_hbm, gw)
    load_mom = load("mom", mom_hbm, mom)
    load_cot.start()

    @pl.when(near)
    def _():
        load_weight.start()

    for one in (load_acts, load_mant, load_expo, load_gw, load_mom):
        one.start()

    def piece(j, plane, k, q):
        return wbuf.at[j, plane, cols[k], pl.ds(q * HALF, HALF)]

    def w_v(i, j, k, q):
        return remote(piece(j, c, k, q), piece(j, c, k, q), wv_s, wv_r, i, dev_v)

    def w_h(i, j, k, q):
        return remote(piece(j, c, k, q), piece(j, c, k, q), wh_s, wh_r, i, dev_h)

    def w_sib(w, k, q):
        j = (ja, jb)[w]
        return remote(piece(j, c, k, q), piece(j, c, k, q), bw_s, bw_r, w * 4 + k * 2 + q, dev_s)

    def w_from_sib(w, k, q):
        j = (ja, jb)[w]
        return remote(piece(j, 1 - c, k, q), piece(j, 1 - c, k, q), bw_s, bw_r, w * 4 + k * 2 + q, dev_s)

    def w_from_z(q):
        return remote(piece(ja, c, 1, q), piece(ja, c, 1, q), z_s, z_r, 1 + q, dev_z)

    def w_to_z(q):
        return remote(
            weight_hbm.at[pl.ds(q * HALF, HALF)], wbuf.at[odd, c, t, pl.ds(q * HALF, HALF)], z_s, z_r, 1 + q, dev_z
        )

    near_v = [(ja, 0, 0), (ja, 1, 0), (ja, 1, 1), (ja, 0, 1), (jb, 0, 1)]
    far_v = [(jb, 0, 0)]
    near_h = [(ja, 0, 1), (ja, 1, 0), (ja, 1, 1)]
    near_h_in = [(jb, 0, 1), (jb, 1, 0), (jb, 1, 1)]
    far_h = [(ja, 0, 0), (ja, 1, 0), (ja, 1, 1)]
    far_h_in = [(jb, 0, 0), (jb, 1, 0), (jb, 1, 1)]

    def part(p, w):
        return gsum.at[p // 2, w, p % 2]

    def g_v(i, src):
        return remote(src, rv.at[i], rv_s, rv_r, i, dev_v)

    def g_h(i, src):
        return remote(src, rh.at[i], rh_s, rh_r, i, dev_h)

    def add_into(dst, src):
        dst[...] = (dst[...].astype(F32) + src[...].astype(F32)).astype(BF16)

    pl.semaphore_wait(barrier, len(everyone))

    send_cot = remote(cot.at[t], cot.at[t], z_s, z_r, 0, dev_z)

    @pl.when(near)
    def _():
        load_weight.wait()
        w_v(0, *near_v[0]).start()
        w_h(0, *near_h[0]).start()
        w_sib(0, 0, 0).start()
        w_sib(0, 0, 1).start()

    @pl.when(far)
    def _():
        w_to_z(0).start()

    load_cot.wait()
    send_cot.start()

    @pl.when(far)
    def _():
        w_to_z(1).start()

    def grad_block(k, w, plane, q):
        at = (ja, jb)[w] * 2 * ROWS + plane * ROWS + q * HALF
        return tt_dot(acts[:, pl.ds(pl.multiple_of(at, HALF), HALF)], cot[cols[k]])

    def grad_send(k, q):
        for w in range(2):
            gsend[k, q, w] = grad_block(k, w, 1 - c, q).astype(BF16)
        copy = remote(gsend.at[k, q], grecv.at[k, q], bg_s, bg_r, k * 2 + q, dev_s)
        copy.start()
        return copy

    def grad_sum(k, q, copy):
        copy.wait_recv()
        for w in range(2):
            gsum[k, w, q] = (grad_block(k, w, c, q) + grecv[k, q, w].astype(F32)).astype(BF16)

    load_acts.wait()
    send_g = {}
    for q in range(2):
        send_g[0, q] = grad_send(0, q)
    grad_sum(0, 0, send_g[0, 0])

    @pl.when(far)
    def _():
        g_v(0, part(0, 1)).start()
        g_v(1, part(0, 0)).start()

    grad_sum(0, 1, send_g[0, 1])

    @pl.when(near)
    def _():
        g_h(1, part(1, 1)).start()

    @pl.when(far)
    def _():
        g_h(0, part(1, 1)).start()

    load_mant.wait()
    load_expo.wait()
    fragment = lax.rem(round_ref[0], FRAGS)
    power = jnp.exp2(expo[fragment].astype(F32))
    power = jnp.transpose(jnp.concatenate([power] * 4, axis=0))
    for h in range(2):
        block = mant[fragment, :, h * 128 : (h + 1) * 128].astype(F32) * power[:, h : h + 1]
        contrib[:, :, :, h * 128 : (h + 1) * 128] = block.astype(BF16).reshape(4, 4, STATE, 128)
    x_sends = [
        remote(contrib.at[:, lax.rem(x + d, 4)], xr.at[d - 1], xs_s, xs_r, d - 1, dev_x[d - 1]) for d in (1, 2, 3)
    ]
    for copy in x_sends:
        copy.start()

    @pl.when(near)
    def _():
        w_from_z(0).wait_recv()
        w_v(1, *near_v[1]).start()
        w_h(1, *near_h[1]).start()
        w_sib(0, 1, 0).start()
        w_h(0, *near_h_in[0]).wait_recv()
        w_sib(1, 0, 1).start()

    @pl.when(far)
    def _():
        w_v(0, *near_v[0]).wait_recv()
        w_h(0, *far_h[0]).start()
        w_sib(0, 0, 0).start()

    remote(cot.at[1 - t], cot.at[1 - t], z_s, z_r, 0, dev_z).wait_recv()
    for q in (1, 0):
        send_g[1, q] = grad_send(1, q)
    grad_sum(1, 1, send_g[1, 1])

    @pl.when(near)
    def _():
        g_v(0, part(3, 1)).start()

    grad_sum(1, 0, send_g[1, 0])

    @pl.when(near)
    def _():
        g_h(2, part(2, 1)).start()

    @pl.when(far)
    def _():
        g_h(1, part(2, 1)).start()

    for copy in x_sends:
        copy.wait_recv()
    for i in range(4):
        total = contrib[i, x].astype(F32)
        for d in range(3):
            total = total + xr[d, i].astype(F32)
        xsum[i] = total.astype(BF16)
    z_sends = [
        remote(xsum.at[lax.rem(zh + d, 4)], zrecv.at[d - 1], zs_s, zs_r, d - 1, dev_zh[d - 1]) for d in (1, 2, 3)
    ]
    for copy in z_sends:
        copy.start()

    @pl.when(near)
    def _():
        w_from_z(1).wait_recv()
        w_v(2, *near_v[2]).start()
        w_h(2, *near_h[2]).start()
        w_v(3, *near_v[3]).start()
        w_v(4, *near_v[4]).start()
        w_sib(0, 1, 1).start()
        w_h(1, *near_h_in[1]).wait_recv()
        w_sib(1, 1, 0).start()
        g_v(0, rv.at[0]).wait_recv()
        add_into(rv.at[0], part(0, 1))
        g_h(0, rv.at[0]).start()

    @pl.when(far)
    def _():
        w_h(0, *far_h_in[0]).wait_recv()
        w_v(0, *far_v[0]).start()
        w_sib(1, 0, 0).start()
        w_v(1, *near_v[1]).wait_recv()
        w_sib(0, 1, 0).start()
        g_v(0, rv.at[0]).wait_recv()
        add_into(rv.at[0], part(3, 1))
        g_h(2, rv.at[0]).start()
        g_h(1, rh.at[1]).wait_recv()
        add_into(rh.at[1], part(2, 0))
        g_v(3, rh.at[1]).start()

    load_gw.wait()
    load_mom.wait()
    for copy in z_sends:
        copy.wait_recv()
    total = xsum[zh].astype(F32)
    for d in range(3):
        total = total + zrecv[d].astype(F32)
    delta = total * (1.0 / 16)
    new_moment = BETA * mom[fragment] + delta
    new_weight = gw[fragment] - RATE * (delta + BETA * new_moment)
    for i in range(FRAGS):
        chosen = fragment == i
        mom_out[i] = jnp.where(chosen, new_moment, mom[i])
        gw_out[i] = jnp.where(chosen, new_weight, gw[i])
    frag[zh, x] = new_weight.astype(BF16)
    za_sends = [remote(frag.at[zh, x], frag.at[zh, x], za_s, za_r, d - 1, dev_zh[d - 1]) for d in (1, 2, 3)]
    for copy in za_sends:
        copy.start()

    @pl.when(far)
    def _():
        w_v(2, *near_v[2]).wait_recv()
        w_h(2, *far_h[2]).start()
        w_h(1, *far_h[1]).start()
        w_sib(0, 1, 1).start()
        g_h(2, rh.at[2]).wait_recv()
        add_into(rh.at[2], part(3, 0))
        g_v(4, rh.at[2]).start()
        g_h(0, rh.at[0]).wait_recv()
        add_into(rh.at[0], part(1, 0))
        g_v(2, rh.at[0]).start()

    for d in (1, 2, 3):
        there = frag.at[lax.rem(zh + 4 - d, 4), x]
        remote(there, there, za_s, za_r, d - 1, dev_zh[d - 1]).wait_recv()
    xa_sends = [remote(frag.at[:, x], frag.at[:, x], xa_s, xa_r, d - 1, dev_x[d - 1]) for d in (1, 2, 3)]
    for copy in xa_sends:
        copy.start()

    def wide(w, plane):
        return pl.ds(pl.multiple_of((ja, jb)[w] * 2 * ROWS + plane * ROWS, ROWS), ROWS)

    def key_term(w, plane, k):
        return jnp.dot(acts[:, wide(w, plane)], wbuf[(ja, jb)[w], plane, cols[k]], preferred_element_type=F32)

    def input_block(w, plane):
        j = (ja, jb)[w]
        for q in range(2):
            rows = pl.ds(q * HALF, HALF)
            total = nt_dot(cot[0], wbuf[j, plane, 0, rows]) + nt_dot(cot[1], wbuf[j, plane, 1, rows])
            at = j * 2 * ROWS + plane * ROWS + q * HALF
            ig_out[:, pl.ds(pl.multiple_of(at, HALF), HALF)] = total.astype(BF16)

    def from_sib(w, k):
        for q in range(2):
            w_from_sib(w, k, q).wait_recv()

    other = 1 - c
    key[1] = key_term(0, c, 1)
    from_sib(0, 1)
    key[1] += key_term(0, other, 1)

    @pl.when(near)
    def _():
        g_v(3, rv.at[3]).wait_recv()
        g_h(2, rh.at[2]).wait_recv()
        add_into(rv.at[3], rh.at[2])
        add_into(rv.at[3], part(2, 0))
        remote(rv.at[3], zr.at[0], z_s, z_r, 4, dev_z).start()
        w_v(0, *far_v[0]).wait_recv()
        w_sib(1, 0, 0).start()
        w_h(2, *near_h_in[2]).wait_recv()
        w_sib(1, 1, 1).start()

    @pl.when(far)
    def _():
        w_v(3, *near_v[3]).wait_recv()
        w_sib(0, 0, 1).start()
        w_h(2, *far_h_in[2]).wait_recv()
        w_sib(1, 1, 1).start()

    from_sib(0, 0)
    key[0] = key_term(0, c, 0)
    key[0] += key_term(0, other, 0)
    input_block(0, c)
    input_block(0, other)

    @pl.when(far)
    def _():
        w_h(1, *far_h_in[1]).wait_recv()
        w_sib(1, 1, 0).start()

    key[1] += key_term(1, c, 1)
    from_sib(1, 1)
    key_send[...] = (key[1] + key_term(1, other, 1)).astype(BF16)
    send_key = remote(key_send, key_recv, z_s, z_r, 3, dev_z)
    send_key.start()

    @pl.when(near)
    def _():
        g_v(4, rv.at[4]).wait_recv()
        add_into(rv.at[4], part(3, 0))
        remote(rv.at[4], zr.at[1], z_s, z_r, 5, dev_z).start()

    @pl.when(far)
    def _():
        w_v(4, *near_v[4]).wait_recv()
        w_sib(1, 0, 1).start()

    key[0] += key_term(1, c, 0)
    input_block(1, c)
    from_sib(1, 0)
    key[0] += key_term(1, other, 0)
    input_block(1, other)

    for d in (1, 2, 3):
        there = frag.at[:, lax.rem(x + 4 - d, 4)]
        remote(there, there, xa_s, xa_r, d - 1, dev_x[d - 1]).wait_recv()
    frag_out[...] = frag[...]

    @pl.when(near)
    def _():
        for q in range(2):
            g_v(1 + q, rv.at[1 + q]).wait_recv()
            g_h(q, rh.at[q]).wait_recv()
            total = rv[1 + q].astype(F32) + rh[q].astype(F32) + gsum[0, 0, q].astype(F32)
            wg_out[q] = total.astype(BF16)

    @pl.when(far)
    def _():
        for q in range(2):
            remote(zr.at[q], zr.at[q], z_s, z_r, 4 + q, dev_z).wait_recv()
            wg_out[q] = zr[q]

    send_key.wait_recv()
    key_out[...] = (key[0] + key_recv[...].astype(F32)).astype(BF16)

    for copy in (send_cot, send_key, *send_g.values(), *x_sends, *z_sends, *za_sends, *xa_sends):
        copy.wait_send()
    for w in range(2):
        for k in range(2):
            for q in range(2):
                w_sib(w, k, q).wait_send()
    for i in range(3):
        g_h(i, rh.at[i]).wait_send()

    @pl.when(near)
    def _():
        for i in range(5):
            w_v(i, *near_v[i]).wait_send()
        for i in range(3):
            w_h(i, *near_h[i]).wait_send()
        g_v(0, rv.at[0]).wait_send()
        for q in range(2):
            remote(rv.at[3 + q], zr.at[q], z_s, z_r, 4 + q, dev_z).wait_send()

    @pl.when(far)
    def _():
        w_v(0, *far_v[0]).wait_send()
        for i in range(3):
            w_h(i, *far_h[i]).wait_send()
        for i in range(5):
            g_v(i, rv.at[i]).wait_send()
        for q in range(2):
            w_to_z(q).wait_send()


def deliver(*refs):
    sem = refs[-1]
    half = len(refs) // 2
    copies = []
    for i in range(half):
        if i == 1:
            for n in range(4):
                rows = pl.ds(n * (TOK // 4), TOK // 4)
                copies.append((refs[i].at[rows], refs[half + i].at[rows]))
        else:
            copies.append((refs[i], refs[half + i]))
    copies = [pltpu.make_async_copy(a, b, sem.at[i]) for i, (a, b) in enumerate(copies)]
    for copy in copies:
        copy.start()
    for copy in copies:
        copy.wait()


def local(
    activations, key_weight, key_cotangent, outer_mantissa, outer_exponent, round_index, global_weight, outer_momentum
):
    vmem = pltpu.VMEM
    dma = lambda n: pltpu.SemaphoreType.DMA((n,))
    exponent = jnp.transpose(outer_exponent[0], (0, 2, 1))
    anywhere = pl.BlockSpec(memory_space=pl.ANY)
    hold = lambda v: pltpu.with_memory_space_constraint(v, pltpu.HBM)
    near_by = pl.BlockSpec(memory_space=pltpu.VMEM)
    outs = pl.pallas_call(
        kernel,
        out_shape=(
            jax.ShapeDtypeStruct((TOK, COLS), BF16),
            jax.ShapeDtypeStruct((TOK, WIDTH), BF16),
            jax.ShapeDtypeStruct((2, HALF, COLS), BF16),
            jax.ShapeDtypeStruct((FRAGS, STATE, COLS), F32),
            jax.ShapeDtypeStruct((FRAGS, STATE, COLS), F32),
            jax.ShapeDtypeStruct((4, 4, STATE, COLS), BF16),
        ),
        in_specs=[anywhere] * 5 + [pl.BlockSpec(memory_space=pltpu.SMEM)] + [anywhere] * 2,
        out_specs=[near_by] * 6,
        scratch_shapes=[
            vmem((TOK, WIDTH), BF16),
            vmem((2, TOK, COLS), BF16),
            vmem((2, 2, 2, ROWS, COLS), BF16),
            vmem((2, 2, 2, HALF, COLS), BF16),
            vmem((2, 2, 2, HALF, COLS), BF16),
            vmem((2, 2, 2, HALF, COLS), BF16),
            vmem((5, HALF, COLS), BF16),
            vmem((3, HALF, COLS), BF16),
            vmem((2, HALF, COLS), BF16),
            vmem((2, TOK, COLS), F32),
            vmem((TOK, COLS), BF16),
            vmem((TOK, COLS), BF16),
            vmem((FRAGS, ROWS, COLS), BF16),
            vmem((FRAGS, 2, ROWS), jnp.int32),
            vmem((4, 4, STATE, COLS), BF16),
            vmem((3, 4, STATE, COLS), BF16),
            vmem((4, STATE, COLS), BF16),
            vmem((3, STATE, COLS), BF16),
            vmem((4, 4, STATE, COLS), BF16),
            vmem((FRAGS, STATE, COLS), F32),
            vmem((FRAGS, STATE, COLS), F32),
            dma(len(LOADS)),
            dma(5), dma(5), dma(3), dma(3), dma(5), dma(5), dma(3), dma(3),
            dma(8), dma(8), dma(4), dma(4), dma(6), dma(6),
            dma(3), dma(3), dma(3), dma(3), dma(3), dma(3), dma(3), dma(3),
        ],
        compiler_params=pltpu.CompilerParams(
            collective_id=0, has_side_effects=True, vmem_limit_bytes=44 * 2**20
        ),
    )(
        hold(activations), hold(key_weight[0]), hold(key_cotangent), hold(outer_mantissa[0]), hold(exponent),
        round_index, hold(global_weight), hold(outer_momentum),
    )
    outs = pl.pallas_call(
        deliver,
        out_shape=tuple(jax.ShapeDtypeStruct(o.shape, o.dtype) for o in outs),
        in_specs=[anywhere] * 6,
        out_specs=[anywhere] * 6,
        scratch_shapes=[dma(9)],
        compiler_params=pltpu.CompilerParams(vmem_limit_bytes=2**20),
    )(*outs)
    key_states, input_grad, weight_grad, global_weight_out, momentum_out, fragment_weight = outs
    return (
        key_states,
        input_grad,
        weight_grad.reshape(1, ROWS, COLS),
        global_weight_out,
        momentum_out,
        fragment_weight.reshape(ROWS, COLS),
    )


def solution(mesh):
    placed = (
        P(("replica", "fsdp"), "tensor"),
        P("replica", "fsdp", "tensor"),
        P(("replica", "fsdp"), "tensor"),
        P("replica", None, "fsdp", "tensor"),
        P("replica", None, "fsdp", "tensor"),
        P(),
        P(None, ("fsdp", "replica"), "tensor"),
        P(None, ("fsdp", "replica"), "tensor"),
    )
    return jax.shard_map(
        local,
        mesh=mesh,
        in_specs=placed,
        out_specs=(
            P(("replica", "fsdp"), "tensor"),
            P(("replica", "fsdp"), "tensor"),
            P("replica", "fsdp", "tensor"),
            P(None, ("fsdp", "replica"), "tensor"),
            P(None, ("fsdp", "replica"), "tensor"),
            P("fsdp", "tensor"),
        ),
        check_vma=False,
    )
```

```python
import jax
import jax.numpy as jnp
from jax import lax
from jax.experimental import pallas as pl
from jax.experimental.pallas import tpu as pltpu
from jax.sharding import PartitionSpec as P

MESH = pl.DeviceIdType.MESH
F32 = jnp.float32
BF16 = jnp.bfloat16

TOK = 384
ROWS = 1024
COLS = 256
WIDTH = 4096
STATE = 64
FRAGS = 4
RATE = 0.7
BETA = 0.9
PIECES = 4
PIECE = ROWS // PIECES
WEIGHT_ROUTE = ((2, 1, 2, 4), (2, 4, 1, 2))
GRAD_ROUTE = ((2, 1, 4, 1), (2, 4, 2, 2))
LOADS = ("cot", "weight", "acts", "mant", "expo", "gw", "mom")

STEPS = (
    "Gs00", "Gs01", "Gs02", "Gs03", "Gk00", "Gk01", "Gk02", "Gk03", "O1",
    "Gs10", "Gs11", "Gs12", "Gs13", "Gk10", "Gk11", "Gk12", "Gk13", "O2", "O3", "Ka0",
    "Ka1", "O4", "Kb", "Kc", "Kd0", "Kd1", "Ke0", "Ke1", "O5", "Kf",
)
NEAR = (
    (
        ("cot", 0, 0, 0), ("s", 0, 0, 1), ("s", 0, 0, 0), ("v", 0, 0, 2), ("s", 0, 0, 2), ("h", 0, 0, 0),
    ),
    (),
    (),
    (),
    (
        ("s", 0, 0, 3), ("v", 0, 0, 3), ("h", 0, 0, 2),
    ),
    (),
    (),
    (),
    (),
    (
        ("gv", 1, 0, 2), ("s", 1, 0, 0),
    ),
    (),
    (),
    (),
    (
        ("gh", 1, 0, 0),
    ),
    (
        ("s", 1, 0, 2),
    ),
    (
        ("gv", 1, 1, 1), ("s", 0, 1, 0),
    ),
    (
        ("gh", 1, 1, 0),
    ),
    (
        ("v", 0, 1, 0), ("s", 0, 1, 1), ("h", 0, 1, 0),
    ),
    (
        ("v", 0, 1, 1), ("s", 0, 1, 2), ("h", 0, 1, 2), ("f", 0, 0, 0), ("s", 1, 1, 0), ("v", 0, 1, 2),
        ("s", 0, 1, 3), ("h", 0, 1, 3), ("f", 0, 1, 0), ("s", 1, 1, 2), ("v", 1, 1, 2), ("gh", 1, 1, 2),
    ),
    (),
    (),
    (
        ("s", 1, 1, 3), ("v", 0, 1, 3), ("gh", 1, 0, 1), ("f", 0, 1, 1), ("v", 0, 0, 1), ("h", 0, 0, 1),
        ("f", 0, 1, 2),
    ),
    (
        ("f", 0, 0, 1), ("v", 0, 0, 0), ("gh", 1, 1, 3), ("s", 1, 1, 1), ("s", 1, 0, 1),
    ),
    (
        ("v", 1, 0, 1),
    ),
    (),
    (),
    (
        ("gh", 1, 0, 3), ("f", 0, 1, 3),
    ),
    (
        ("s", 1, 0, 3), ("f", 0, 0, 3),
    ),
    (),
    (),
    (
        ("f", 0, 0, 2),
    ),
)
FAR = (
    (
        ("cot", 0, 0, 0),
    ),
    (),
    (),
    (),
    (),
    (
        ("gh", 1, 0, 0),
    ),
    (
        ("gv", 1, 0, 1), ("z", 0, 1, 0),
    ),
    (),
    (),
    (
        ("h", 0, 0, 2), ("s", 0, 0, 2),
    ),
    (),
    (),
    (),
    (
        ("gv", 0, 0, 3), ("z", 0, 1, 1),
    ),
    (
        ("s", 0, 0, 3),
    ),
    (
        ("gh", 1, 1, 0),
    ),
    (
        ("gv", 0, 0, 1),
    ),
    (
        ("z", 0, 1, 2), ("s", 1, 0, 2), ("gh", 1, 1, 2), ("gv", 0, 0, 0), ("z", 0, 1, 3),
    ),
    (
        ("gh", 1, 1, 1), ("gv", 0, 1, 0), ("s", 0, 1, 0), ("gh", 1, 1, 3), ("gv", 0, 1, 2), ("s", 0, 1, 1),
        ("h", 0, 1, 1), ("gv", 0, 1, 1),
    ),
    (
        ("s", 0, 1, 2), ("h", 0, 1, 0), ("gv", 0, 1, 3), ("f", 0, 1, 0), ("s", 1, 1, 1), ("s", 1, 1, 2),
        ("h", 0, 0, 3), ("v", 1, 1, 1), ("s", 1, 1, 0), ("s", 0, 1, 3),
    ),
    (
        ("h", 0, 1, 3), ("gv", 1, 0, 3),
    ),
    (),
    (
        ("f", 0, 1, 1), ("s", 1, 0, 3), ("s", 0, 0, 1), ("gh", 1, 0, 2), ("v", 1, 0, 3), ("f", 0, 1, 2),
        ("s", 1, 1, 3),
    ),
    (
        ("s", 0, 0, 0), ("h", 0, 0, 0),
    ),
    (),
    (),
    (
        ("gv", 0, 0, 2), ("s", 1, 0, 1), ("s", 1, 0, 0),
    ),
    (),
    (),
    (),
    (
        ("f", 0, 1, 3),
    ),
)


def tt_dot(a, b):
    return lax.dot_general(a, b, (((0,), (0,)), ((), ())), preferred_element_type=F32)


def nt_dot(a, b):
    return lax.dot_general(a, b, (((1,), (1,)), ((), ())), preferred_element_type=F32)


def kernel(
    acts_hbm, weight_hbm, cot_hbm, mant_hbm, expo_hbm, round_ref, gw_hbm, mom_hbm,
    key_out, ig_out, wg_out, gw_out, mom_out, frag_out,
    acts, cot, wbuf, gsend, grecv, gsum, rv, rh, zr, key, key_send, key_recv,
    mant, expo, contrib, xr, xsum, zrecv, frag, gw, mom,
    ld, wv_s, wv_r, wh_s, wh_r, rv_s, rv_r, rh_s, rh_r, bw_s, bw_r, bg_s, bg_r, z_s, z_r,
    xs_s, xs_r, zs_s, zs_r, za_s, za_r, xa_s, xa_r,
):
    r = lax.axis_index("replica")
    f = lax.axis_index("fsdp")
    t = lax.axis_index("tensor")
    zh, x = r // 4, lax.rem(r, 4)
    y, c = f // 2, lax.rem(f, 2)
    odd = lax.rem(y, 2)
    near = (y // 2) == t
    far = (y // 2) != t
    ja = jnp.where(near, odd, 1 - odd)
    column = (ja, 1 - ja)
    cols = (t, 1 - t)
    dev_h = (r, (y + 1 - 2 * odd) * 2 + c, t)
    dev_v = (r, (3 - y) * 2 + c, t)
    dev_z = (r, f, 1 - t)
    dev_s = (r, y * 2 + 1 - c, t)
    dev_x = [(zh * 4 + lax.rem(x + d, 4), f, t) for d in (1, 2, 3)]
    dev_zh = [(lax.rem(zh + d, 4) * 4 + x, f, t) for d in (1, 2, 3)]

    barrier = pltpu.get_barrier_semaphore()
    everyone = [dev_h, dev_v, dev_z, dev_s, *dev_x, *dev_zh]
    for device in everyone:
        pl.semaphore_signal(barrier, inc=1, device_id=device, device_id_type=MESH)

    def load(name, src, dst):
        return pltpu.make_async_copy(src, dst, ld.at[LOADS.index(name)])

    def remote(src, dst, s, r_, i, device):
        return pltpu.make_async_remote_copy(
            src_ref=src, dst_ref=dst, send_sem=s.at[i], recv_sem=r_.at[i], device_id=device, device_id_type=MESH
        )

    load_cot = load("cot", cot_hbm, cot.at[t])
    load_weight = load("weight", weight_hbm, wbuf.at[ja, c, t])
    load_acts = load("acts", acts_hbm, acts)
    load_mant = load("mant", mant_hbm, mant)
    load_expo = load("expo", expo_hbm, expo)
    load_gw = load("gw", gw_hbm, gw)
    load_mom = load("mom", mom_hbm, mom)
    load_cot.start()

    @pl.when(near)
    def _():
        load_weight.start()

    for one in (load_acts, load_mant, load_expo, load_gw, load_mom):
        one.start()

    def piece(w, plane, k, q):
        return wbuf.at[column[w], plane, cols[k], pl.ds(q * PIECE, PIECE)]

    def at(w, k, q):
        return (w * 2 + k) * PIECES + q

    def part(w, k, q):
        return gsum.at[k, w, q]

    def from_sib(w, k, q):
        there = piece(w, 1 - c, k, q)
        return remote(there, there, bw_s, bw_r, at(w, k, q), dev_s)

    def copy_of(name, w, k, q):
        if name == "v":
            return remote(piece(w, c, k, q), piece(w, c, k, q), wv_s, wv_r, at(w, k, q), dev_v)
        if name == "h":
            return remote(piece(w, c, k, q), piece(w, c, k, q), wh_s, wh_r, at(0, k, q), dev_h)
        if name == "s":
            return remote(piece(w, c, k, q), piece(w, c, k, q), bw_s, bw_r, at(w, k, q), dev_s)
        if name == "z":
            rows = pl.ds(q * PIECE, PIECE)
            return remote(weight_hbm.at[rows], wbuf.at[odd, c, t, rows], z_s, z_r, 2 + q, dev_z)
        if name == "gv":
            src = part(w, k, q)
            if w == 0 and GRAD_ROUTE[k][q] != 1:
                src = rh.at[k, q]
            return remote(src, rv.at[w, k, q], rv_s, rv_r, at(w, k, q), dev_v)
        if name == "f":
            return remote(rv.at[0, k, q], zr.at[q], z_s, z_r, 2 + PIECES + q, dev_z)
        return remote(cot.at[t], cot.at[t], z_s, z_r, 0, dev_z)

    def grad_h(is_near, k, q):
        route = GRAD_ROUTE[k][q]
        src = rv.at[1, k, q] if route == (1 if is_near else 4) else part(1, k, q)
        return remote(src, rh.at[k, q], rh_s, rh_r, at(0, k, q), dev_h)

    def add_into(dst, *others):
        total = dst[...].astype(F32)
        for other in others:
            total = total + other[...].astype(F32)
        dst[...] = total.astype(BF16)

    class Role:
        def __init__(self, is_near):
            self.is_near = is_near
            self.seen = set()

        def once(self, key, *copy):
            if key not in self.seen:
                self.seen.add(key)
                remote(*copy).wait_recv()

        def have(self, w, k, q):
            there = piece(w, c, k, q)
            if self.is_near and w == 0:
                if k == 0:
                    if "weight" not in self.seen:
                        self.seen.add("weight")
                        load_weight.wait()
                else:
                    self.once(("z", q), there, there, z_s, z_r, 2 + q, dev_z)
                return
            over_v = (WEIGHT_ROUTE[k][q] == 4) if self.is_near else (w == 0 or WEIGHT_ROUTE[k][q] == 1)
            if over_v:
                self.once(("v", w, k, q), there, there, wv_s, wv_r, at(w, k, q), dev_v)
            else:
                self.once(("h", w, k, q), there, there, wh_s, wh_r, at(0, k, q), dev_h)

        def have_v(self, w, k, q):
            there = rv.at[w, k, q]
            self.once(("gv", w, k, q), there, there, rv_s, rv_r, at(w, k, q), dev_v)

        def have_h(self, k, q):
            there = rh.at[k, q]
            self.once(("gh", k, q), there, there, rh_s, rh_r, at(0, k, q), dev_h)

        def copy(self, name, w, k, q):
            return grad_h(self.is_near, k, q) if name == "gh" else copy_of(name, w, k, q)

        def do(self, name, w, k, q):
            if name in ("v", "h", "s"):
                self.have(w, k, q)
            elif name == "cot":
                load_cot.wait()
            elif name == "gh":
                if GRAD_ROUTE[k][q] == (1 if self.is_near else 4):
                    self.have_v(1, k, q)
                    add_into(rv.at[1, k, q], part(1, k, q))
            elif name == "gv":
                if w == 0 and GRAD_ROUTE[k][q] != 1:
                    self.have_h(k, q)
                    add_into(rh.at[k, q], part(0, k, q))
            elif name == "f":
                if not self.is_near:
                    remote(zr.at[q], zr.at[q], z_s, z_r, 2 + PIECES + q, dev_z).wait_recv()
                    wg_out[q] = zr[q]
                    return
                self.have_v(0, k, q)
                terms = [part(0, k, q)]
                if GRAD_ROUTE[k][q] != 4:
                    self.have_h(k, q)
                    terms.append(rh.at[k, q])
                add_into(rv.at[0, k, q], *terms)
                if k == 0:
                    wg_out[q] = rv[0, k, q]
                    return
            self.copy(name, w, k, q).start()

        def sent(self, name, w, k, q):
            return not (name == "f" and (k == 0 or not self.is_near))

    roles = ((near, Role(True), NEAR), (far, Role(False), FAR))
    chosen = lax.rem(round_ref[0], FRAGS)
    other = 1 - c

    def grad_block(k, w, plane, q):
        first = column[w] * 2 * ROWS + plane * ROWS + q * PIECE
        return tt_dot(acts[:, pl.ds(pl.multiple_of(first, PIECE), PIECE)], cot[cols[k]])

    def grad_to_sib(k, q):
        return remote(gsend.at[k, q], grecv.at[k, q], bg_s, bg_r, k * PIECES + q, dev_s)

    def grad_send(k, q):
        if (k, q) == (0, 0):
            load_acts.wait()
        if (k, q) == (1, 0):
            remote(cot.at[1 - t], cot.at[1 - t], z_s, z_r, 0, dev_z).wait_recv()
        for w in range(2):
            gsend[k, q, w] = grad_block(k, w, other, q).astype(BF16)
        grad_to_sib(k, q).start()

    def grad_keep(k, q):
        grad_to_sib(k, q).wait_recv()
        for w in range(2):
            gsum[k, w, q] = (grad_block(k, w, c, q) + grecv[k, q, w].astype(F32)).astype(BF16)

    def x_send(d):
        return remote(contrib.at[:, lax.rem(x + d, 4)], xr.at[d - 1], xs_s, xs_r, d - 1, dev_x[d - 1])

    def z_send(d):
        return remote(xsum.at[lax.rem(zh + d, 4)], zrecv.at[d - 1], zs_s, zs_r, d - 1, dev_zh[d - 1])

    def z_back(d):
        return remote(frag.at[zh, x], frag.at[zh, x], za_s, za_r, d - 1, dev_zh[d - 1])

    def x_back(d):
        return remote(frag.at[:, x], frag.at[:, x], xa_s, xa_r, d - 1, dev_x[d - 1])

    def outer_1():
        load_mant.wait()
        load_expo.wait()
        power = jnp.exp2(expo[chosen].astype(F32))
        power = jnp.transpose(jnp.concatenate([power] * 4, axis=0))
        for h in range(2):
            block = mant[chosen, :, h * 128 : (h + 1) * 128].astype(F32) * power[:, h : h + 1]
            contrib[:, :, :, h * 128 : (h + 1) * 128] = block.astype(BF16).reshape(4, 4, STATE, 128)
        for d in (1, 2, 3):
            x_send(d).start()

    def outer_2():
        for d in (1, 2, 3):
            x_send(d).wait_recv()
        for i in range(4):
            total = contrib[i, x].astype(F32)
            for d in range(3):
                total = total + xr[d, i].astype(F32)
            xsum[i] = total.astype(BF16)
        for d in (1, 2, 3):
            z_send(d).start()

    def outer_3():
        load_gw.wait()
        load_mom.wait()
        for d in (1, 2, 3):
            z_send(d).wait_recv()
        total = xsum[zh].astype(F32)
        for d in range(3):
            total = total + zrecv[d].astype(F32)
        delta = total * (1.0 / 16)
        new_moment = BETA * mom[chosen] + delta
        new_weight = gw[chosen] - RATE * (delta + BETA * new_moment)
        for i in range(FRAGS):
            mom_out[i] = jnp.where(chosen == i, new_moment, mom[i])
            gw_out[i] = jnp.where(chosen == i, new_weight, gw[i])
        frag[zh, x] = new_weight.astype(BF16)
        for d in (1, 2, 3):
            z_back(d).start()

    def outer_4():
        for d in (1, 2, 3):
            there = frag.at[lax.rem(zh + 4 - d, 4), x]
            remote(there, there, za_s, za_r, d - 1, dev_zh[d - 1]).wait_recv()
        for d in (1, 2, 3):
            x_back(d).start()

    def outer_5():
        for d in (1, 2, 3):
            there = frag.at[:, lax.rem(x + 4 - d, 4)]
            remote(there, there, xa_s, xa_r, d - 1, dev_x[d - 1]).wait_recv()
        frag_out[...] = frag[...]

    def key_term(w, plane, k):
        wide = pl.ds(pl.multiple_of(column[w] * 2 * ROWS + plane * ROWS, ROWS), ROWS)
        return jnp.dot(acts[:, wide], wbuf[column[w], plane, cols[k]], preferred_element_type=F32)

    def input_block(w, plane):
        for i in range(2):
            rows = pl.ds(i * 512, 512)
            total = nt_dot(cot[0], wbuf[column[w], plane, 0, rows]) + nt_dot(cot[1], wbuf[column[w], plane, 1, rows])
            first = column[w] * 2 * ROWS + plane * ROWS + i * 512
            ig_out[:, pl.ds(pl.multiple_of(first, 512), 512)] = total.astype(BF16)

    def sib_pieces(w, k):
        for q in range(PIECES):
            from_sib(w, k, q).wait_recv()

    send_key = remote(key_send, key_recv, z_s, z_r, 1, dev_z)

    def step(name):
        if name[0] == "G":
            (grad_send if name[1] == "s" else grad_keep)(int(name[2]), int(name[3]))
        elif name[0] == "O":
            (outer_1, outer_2, outer_3, outer_4, outer_5)[int(name[1]) - 1]()
        elif name == "Ka0":
            key[1] = key_term(0, c, 1)
        elif name == "Ka1":
            sib_pieces(0, 1)
            key[1] += key_term(0, other, 1)
        elif name == "Kb":
            key[1] += key_term(1, c, 1)
        elif name == "Kc":
            sib_pieces(1, 1)
            key_send[...] = (key[1] + key_term(1, other, 1)).astype(BF16)
            send_key.start()
        elif name == "Kd0":
            key[0] = key_term(0, c, 0)
            input_block(0, c)
        elif name == "Kd1":
            sib_pieces(0, 0)
            key[0] += key_term(0, other, 0)
            input_block(0, other)
        elif name == "Ke0":
            key[0] += key_term(1, c, 0)
            input_block(1, c)
        elif name == "Ke1":
            sib_pieces(1, 0)
            key[0] += key_term(1, other, 0)
            input_block(1, other)
        else:
            send_key.wait_recv()
            key_out[...] = (key[0] + key_recv[...].astype(F32)).astype(BF16)

    own_pieces = {"Ka0": (0, 1), "Kb": (1, 1), "Kd0": (0, 0), "Ke0": (1, 0)}

    pl.semaphore_wait(barrier, len(everyone))
    for i, name in enumerate((*STEPS, None)):
        for here, role, plan in roles:

            @pl.when(here)
            def _(role=role, tasks=plan[i], name=name):
                for task in tasks:
                    role.do(*task)
                if name in own_pieces:
                    for q in range(PIECES):
                        role.have(*own_pieces[name], q)

        if name is not None:
            step(name)

    send_key.wait_send()
    for d in (1, 2, 3):
        for copy in (x_send(d), z_send(d), z_back(d), x_back(d)):
            copy.wait_send()
    for k in range(2):
        for q in range(PIECES):
            grad_to_sib(k, q).wait_send()
    for here, role, plan in roles:

        @pl.when(here)
        def _(role=role, plan=plan):
            for tasks in plan:
                for task in tasks:
                    if role.sent(*task):
                        role.copy(*task).wait_send()


def deliver(*refs):
    sem = refs[-1]
    half = len(refs) // 2
    pairs = list(zip(refs[:half], refs[half:-1]))
    ig, ig_out = pairs.pop(1)
    quarter = TOK // 4
    for n in range(4):
        rows = pl.ds(n * quarter, quarter)
        pairs.append((ig.at[rows], ig_out.at[rows]))
    copies = [pltpu.make_async_copy(a, b, sem.at[i]) for i, (a, b) in enumerate(pairs)]
    for copy in copies:
        copy.start()
    for copy in copies:
        copy.wait()


def local(
    activations, key_weight, key_cotangent, outer_mantissa, outer_exponent, round_index, global_weight, outer_momentum
):
    vmem = pltpu.VMEM
    dma = lambda n: pltpu.SemaphoreType.DMA((n,))
    hold = lambda v: pltpu.with_memory_space_constraint(v, pltpu.HBM)
    exponent = jnp.transpose(outer_exponent[0], (0, 2, 1))
    anywhere = pl.BlockSpec(memory_space=pl.ANY)
    near_by = pl.BlockSpec(memory_space=pltpu.VMEM)
    n = PIECES
    outs = pl.pallas_call(
        kernel,
        out_shape=(
            jax.ShapeDtypeStruct((TOK, COLS), BF16),
            jax.ShapeDtypeStruct((TOK, WIDTH), BF16),
            jax.ShapeDtypeStruct((n, PIECE, COLS), BF16),
            jax.ShapeDtypeStruct((FRAGS, STATE, COLS), F32),
            jax.ShapeDtypeStruct((FRAGS, STATE, COLS), F32),
            jax.ShapeDtypeStruct((4, 4, STATE, COLS), BF16),
        ),
        in_specs=[anywhere] * 5 + [pl.BlockSpec(memory_space=pltpu.SMEM)] + [anywhere] * 2,
        out_specs=[near_by] * 6,
        scratch_shapes=[
            vmem((TOK, WIDTH), BF16),
            vmem((2, TOK, COLS), BF16),
            vmem((2, 2, 2, ROWS, COLS), BF16),
            vmem((2, n, 2, PIECE, COLS), BF16),
            vmem((2, n, 2, PIECE, COLS), BF16),
            vmem((2, 2, n, PIECE, COLS), BF16),
            vmem((2, 2, n, PIECE, COLS), BF16),
            vmem((2, n, PIECE, COLS), BF16),
            vmem((n, PIECE, COLS), BF16),
            vmem((2, TOK, COLS), F32),
            vmem((TOK, COLS), BF16),
            vmem((TOK, COLS), BF16),
            vmem((FRAGS, ROWS, COLS), BF16),
            vmem((FRAGS, 2, ROWS), jnp.int32),
            vmem((4, 4, STATE, COLS), BF16),
            vmem((3, 4, STATE, COLS), BF16),
            vmem((4, STATE, COLS), BF16),
            vmem((3, STATE, COLS), BF16),
            vmem((4, 4, STATE, COLS), BF16),
            vmem((FRAGS, STATE, COLS), F32),
            vmem((FRAGS, STATE, COLS), F32),
            dma(len(LOADS)),
            dma(4 * n), dma(4 * n), dma(2 * n), dma(2 * n), dma(4 * n), dma(4 * n), dma(2 * n), dma(2 * n),
            dma(4 * n), dma(4 * n), dma(2 * n), dma(2 * n), dma(2 + 2 * n), dma(2 + 2 * n),
            dma(3), dma(3), dma(3), dma(3), dma(3), dma(3), dma(3), dma(3),
        ],
        compiler_params=pltpu.CompilerParams(
            collective_id=0, has_side_effects=True, vmem_limit_bytes=44 * 2**20
        ),
    )(
        hold(activations), hold(key_weight[0]), hold(key_cotangent), hold(outer_mantissa[0]), hold(exponent),
        round_index, hold(global_weight), hold(outer_momentum),
    )
    outs = pl.pallas_call(
        deliver,
        out_shape=tuple(jax.ShapeDtypeStruct(o.shape, o.dtype) for o in outs),
        in_specs=[anywhere] * 6,
        out_specs=[anywhere] * 6,
        scratch_shapes=[dma(9)],
        compiler_params=pltpu.CompilerParams(vmem_limit_bytes=2**20),
    )(*outs)
    key_states, input_grad, weight_grad, global_weight_out, momentum_out, fragment_weight = outs
    return (
        key_states,
        input_grad,
        weight_grad.reshape(1, ROWS, COLS),
        global_weight_out,
        momentum_out,
        fragment_weight.reshape(ROWS, COLS),
    )


def solution(mesh):
    placed = (
        P(("replica", "fsdp"), "tensor"),
        P("replica", "fsdp", "tensor"),
        P(("replica", "fsdp"), "tensor"),
        P("replica", None, "fsdp", "tensor"),
        P("replica", None, "fsdp", "tensor"),
        P(),
        P(None, ("fsdp", "replica"), "tensor"),
        P(None, ("fsdp", "replica"), "tensor"),
    )
    return jax.shard_map(
        local,
        mesh=mesh,
        in_specs=placed,
        out_specs=(
            P(("replica", "fsdp"), "tensor"),
            P(("replica", "fsdp"), "tensor"),
            P("replica", "fsdp", "tensor"),
            P(None, ("fsdp", "replica"), "tensor"),
            P(None, ("fsdp", "replica"), "tensor"),
            P("fsdp", "tensor"),
        ),
        check_vma=False,
    )
```

```python
import jax
import jax.numpy as jnp
from jax import lax
from jax.experimental import pallas as pl
from jax.experimental.pallas import tpu as pltpu
from jax.sharding import PartitionSpec as P

MESH = pl.DeviceIdType.MESH
F32 = jnp.float32
BF16 = jnp.bfloat16

TOK = 384
ROWS = 1024
COLS = 256
WIDTH = 4096
STATE = 64
FRAGS = 4
RATE = 0.7
BETA = 0.9
PIECES = 4
PIECE = ROWS // PIECES
WEIGHT_ROUTE = ((1, 4, 4, 2), (1, 2, 2, 2))
GRAD_ROUTE = ((2, 2, 4, 1), (2, 2, 1, 4))
LOADS = ("cot", "weight", "acts", "mant", "expo", "gw", "mom")

STEPS = (
    "Gs00", "Gs01", "Gs02", "Gs03", "O1", "Gk00", "Gk01", "Gk02", "Gk03",
    "Gs10", "Gs11", "Gs12", "Gs13", "Gk10", "Gk11", "Gk12", "Gk13", "O2", "Ka0", "Ka1",
    "O3", "Kb", "Kc", "O4", "Kd0", "Kd1", "Ke0", "Ke1", "O5", "Kf",
)
NEAR = (
    (
        ("cot", 0, 0, 0), ("s", 0, 0, 3), ("s", 0, 0, 2), ("h", 0, 0, 0), ("s", 0, 0, 1), ("s", 0, 0, 0),
    ),
    (),
    (),
    (),
    (),
    (
        ("v", 0, 0, 1), ("h", 0, 0, 3),
    ),
    (
        ("v", 0, 0, 2),
    ),
    (
        ("gh", 1, 0, 0),
    ),
    (),
    (
        ("s", 1, 0, 0),
    ),
    (),
    (),
    (),
    (
        ("gv", 1, 0, 2), ("gh", 1, 0, 1),
    ),
    (
        ("s", 1, 0, 3),
    ),
    (
        ("s", 0, 1, 0),
    ),
    (),
    (
        ("v", 0, 1, 0), ("gh", 1, 1, 0),
    ),
    (
        ("s", 0, 1, 3), ("v", 0, 1, 3), ("h", 0, 1, 3), ("s", 0, 1, 1), ("f", 0, 0, 0), ("v", 0, 1, 1),
        ("h", 0, 1, 0),
    ),
    (
        ("f", 0, 0, 1), ("s", 0, 1, 2), ("v", 0, 1, 2), ("h", 0, 1, 2),
    ),
    (
        ("s", 1, 1, 3), ("s", 1, 0, 1), ("gv", 1, 1, 3), ("h", 0, 1, 1), ("s", 1, 1, 0),
    ),
    (
        ("f", 0, 1, 0), ("v", 1, 1, 0), ("gh", 1, 1, 1), ("s", 1, 1, 2), ("v", 0, 0, 3), ("gh", 1, 1, 2),
    ),
    (
        ("s", 1, 1, 1), ("f", 0, 0, 2), ("v", 1, 0, 0),
    ),
    (
        ("gh", 1, 0, 3), ("f", 0, 1, 1), ("v", 0, 0, 0),
    ),
    (),
    (),
    (),
    (
        ("f", 0, 0, 3), ("s", 1, 0, 2), ("f", 0, 1, 2),
    ),
    (
        ("f", 0, 1, 3),
    ),
    (),
    (),
)
FAR = (
    (
        ("cot", 0, 0, 0),
    ),
    (),
    (),
    (),
    (),
    (),
    (
        ("gh", 1, 0, 0),
    ),
    (
        ("gh", 1, 0, 1),
    ),
    (
        ("z", 0, 1, 0),
    ),
    (
        ("gv", 0, 0, 3), ("z", 0, 1, 3), ("gv", 1, 0, 3),
    ),
    (),
    (),
    (),
    (
        ("h", 0, 0, 1), ("s", 0, 0, 1),
    ),
    (
        ("gv", 0, 0, 0),
    ),
    (
        ("z", 0, 1, 1),
    ),
    (),
    (
        ("gh", 1, 1, 0), ("s", 0, 0, 2), ("z", 0, 1, 2), ("gv", 0, 0, 1),
    ),
    (
        ("h", 0, 0, 2), ("s", 1, 0, 1), ("v", 1, 0, 1), ("gh", 1, 0, 2), ("s", 0, 1, 0), ("gv", 0, 1, 0),
        ("gh", 1, 1, 1), ("s", 0, 1, 3), ("s", 1, 0, 2), ("gv", 1, 1, 2), ("h", 0, 1, 3), ("s", 0, 1, 1),
        ("gv", 0, 0, 2), ("h", 0, 1, 1), ("s", 0, 1, 2),
    ),
    (
        ("gv", 0, 1, 1),
    ),
    (),
    (
        ("h", 0, 1, 2), ("s", 1, 1, 3), ("v", 1, 0, 2), ("gh", 1, 1, 3), ("f", 0, 1, 0), ("s", 1, 1, 0),
        ("s", 1, 1, 1), ("gv", 0, 1, 2), ("h", 0, 0, 3), ("s", 0, 0, 3),
    ),
    (
        ("s", 1, 1, 2),
    ),
    (
        ("s", 1, 0, 0), ("gv", 0, 1, 3),
    ),
    (
        ("f", 0, 1, 1),
    ),
    (
        ("s", 0, 0, 0), ("s", 1, 0, 3),
    ),
    (),
    (),
    (
        ("f", 0, 1, 2), ("f", 0, 1, 3),
    ),
    (),
    (),
)


def tt_dot(a, b):
    return lax.dot_general(a, b, (((0,), (0,)), ((), ())), preferred_element_type=F32)


def nt_dot(a, b):
    return lax.dot_general(a, b, (((1,), (1,)), ((), ())), preferred_element_type=F32)


def kernel(
    acts_hbm, weight_hbm, cot_hbm, mant_hbm, expo_hbm, round_ref, gw_hbm, mom_hbm,
    key_out, ig_out, wg_out, gw_out, mom_out, frag_out,
    acts, cot, wbuf, gsend, grecv, gsum, rv, rh, zr, key, key_send, key_recv,
    mant, expo, contrib, xr, xsum, zrecv, frag, gw, mom,
    ld, wv_s, wv_r, wh_s, wh_r, rv_s, rv_r, rh_s, rh_r, bw_s, bw_r, bg_s, bg_r, z_s, z_r,
    xs_s, xs_r, zs_s, zs_r, za_s, za_r, xa_s, xa_r, group_sem, go_sem, far_sem,
):
    r = lax.axis_index("replica")
    f = lax.axis_index("fsdp")
    t = lax.axis_index("tensor")
    zh, x = r // 4, lax.rem(r, 4)
    y, c = f // 2, lax.rem(f, 2)
    odd = lax.rem(y, 2)
    near = (y // 2) == t
    far = (y // 2) != t
    ja = jnp.where(near, odd, 1 - odd)
    column = (ja, 1 - ja)
    cols = (t, 1 - t)
    dev_h = (r, (y + 1 - 2 * odd) * 2 + c, t)
    dev_v = (r, (3 - y) * 2 + c, t)
    dev_z = (r, f, 1 - t)
    dev_s = (r, y * 2 + 1 - c, t)
    dev_x = [(zh * 4 + lax.rem(x + d, 4), f, t) for d in (1, 2, 3)]
    dev_zh = [(lax.rem(zh + d, 4) * 4 + x, f, t) for d in (1, 2, 3)]

    barrier = pltpu.get_barrier_semaphore()

    def tell(sem, *devices):
        for device in devices:
            pl.semaphore_signal(sem, inc=1, device_id=device, device_id_type=MESH)

    @pl.when(c == 0)
    def _():
        tell(barrier, dev_h, dev_v, dev_z, *dev_x)

    @pl.when(c == 1)
    def _():
        tell(barrier, dev_s)

    def load(name, src, dst):
        return pltpu.make_async_copy(src, dst, ld.at[LOADS.index(name)])

    def remote(src, dst, s, r_, i, device):
        return pltpu.make_async_remote_copy(
            src_ref=src, dst_ref=dst, send_sem=s.at[i], recv_sem=r_.at[i], device_id=device, device_id_type=MESH
        )

    load_cot = load("cot", cot_hbm, cot.at[t])
    load_weight = load("weight", weight_hbm, wbuf.at[ja, c, t])
    load_acts = load("acts", acts_hbm, acts)
    load_mant = load("mant", mant_hbm, mant)
    load_expo = load("expo", expo_hbm, expo)
    load_gw = load("gw", gw_hbm, gw)
    load_mom = load("mom", mom_hbm, mom)
    load_cot.start()

    @pl.when(near)
    def _():
        load_weight.start()

    for one in (load_acts, load_mant, load_expo, load_gw, load_mom):
        one.start()

    def piece(w, plane, k, q):
        return wbuf.at[column[w], plane, cols[k], pl.ds(q * PIECE, PIECE)]

    def at(w, k, q):
        return (w * 2 + k) * PIECES + q

    def part(w, k, q):
        return gsum.at[k, w, q]

    def from_sib(w, k, q):
        there = piece(w, 1 - c, k, q)
        return remote(there, there, bw_s, bw_r, at(w, k, q), dev_s)

    def copy_of(name, w, k, q):
        if name == "v":
            return remote(piece(w, c, k, q), piece(w, c, k, q), wv_s, wv_r, at(w, k, q), dev_v)
        if name == "h":
            return remote(piece(w, c, k, q), piece(w, c, k, q), wh_s, wh_r, at(0, k, q), dev_h)
        if name == "s":
            return remote(piece(w, c, k, q), piece(w, c, k, q), bw_s, bw_r, at(w, k, q), dev_s)
        if name == "z":
            rows = pl.ds(q * PIECE, PIECE)
            return remote(weight_hbm.at[rows], wbuf.at[odd, c, t, rows], z_s, z_r, 2 + q, dev_z)
        if name == "gv":
            src = part(w, k, q)
            if w == 0 and GRAD_ROUTE[k][q] != 1:
                src = rh.at[k, q]
            return remote(src, rv.at[w, k, q], rv_s, rv_r, at(w, k, q), dev_v)
        if name == "f":
            return remote(rv.at[0, k, q], zr.at[q], z_s, z_r, 2 + PIECES + q, dev_z)
        return remote(cot.at[t], cot.at[t], z_s, z_r, 0, dev_z)

    def grad_h(is_near, k, q):
        route = GRAD_ROUTE[k][q]
        src = rv.at[1, k, q] if route == (1 if is_near else 4) else part(1, k, q)
        return remote(src, rh.at[k, q], rh_s, rh_r, at(0, k, q), dev_h)

    def add_into(dst, *others):
        total = dst[...].astype(F32)
        for other in others:
            total = total + other[...].astype(F32)
        dst[...] = total.astype(BF16)

    class Role:
        def __init__(self, is_near):
            self.is_near = is_near
            self.seen = set()

        def once(self, key, *copy):
            if key not in self.seen:
                self.seen.add(key)
                remote(*copy).wait_recv()

        def have(self, w, k, q):
            there = piece(w, c, k, q)
            if self.is_near and w == 0:
                if k == 0:
                    if "weight" not in self.seen:
                        self.seen.add("weight")
                        load_weight.wait()
                else:
                    self.once(("z", q), there, there, z_s, z_r, 2 + q, dev_z)
                return
            over_v = (WEIGHT_ROUTE[k][q] == 4) if self.is_near else (w == 0 or WEIGHT_ROUTE[k][q] == 1)
            if over_v:
                self.once(("v", w, k, q), there, there, wv_s, wv_r, at(w, k, q), dev_v)
            else:
                self.once(("h", w, k, q), there, there, wh_s, wh_r, at(0, k, q), dev_h)

        def have_v(self, w, k, q):
            there = rv.at[w, k, q]
            self.once(("gv", w, k, q), there, there, rv_s, rv_r, at(w, k, q), dev_v)

        def have_h(self, k, q):
            there = rh.at[k, q]
            self.once(("gh", k, q), there, there, rh_s, rh_r, at(0, k, q), dev_h)

        def copy(self, name, w, k, q):
            return grad_h(self.is_near, k, q) if name == "gh" else copy_of(name, w, k, q)

        def do(self, name, w, k, q):
            if name in ("v", "h", "s"):
                self.have(w, k, q)
            elif name == "cot":
                pass
            elif name == "gh":
                if GRAD_ROUTE[k][q] == (1 if self.is_near else 4):
                    self.have_v(1, k, q)
                    add_into(rv.at[1, k, q], part(1, k, q))
            elif name == "gv":
                if w == 0 and GRAD_ROUTE[k][q] != 1:
                    self.have_h(k, q)
                    add_into(rh.at[k, q], part(0, k, q))
            elif name == "f":
                if not self.is_near:
                    remote(zr.at[q], zr.at[q], z_s, z_r, 2 + PIECES + q, dev_z).wait_recv()
                    wg_out[q] = zr[q]
                    return
                self.have_v(0, k, q)
                terms = [part(0, k, q)]
                if GRAD_ROUTE[k][q] != 4:
                    self.have_h(k, q)
                    terms.append(rh.at[k, q])
                add_into(rv.at[0, k, q], *terms)
                if k == 0:
                    wg_out[q] = rv[0, k, q]
                    return
            self.copy(name, w, k, q).start()

        def sent(self, name, w, k, q):
            return not (name == "f" and (k == 0 or not self.is_near))

    roles = ((near, Role(True), NEAR), (far, Role(False), FAR))
    chosen = lax.rem(round_ref[0], FRAGS)
    other = 1 - c

    def grad_block(k, w, plane, q):
        first = column[w] * 2 * ROWS + plane * ROWS + q * PIECE
        return tt_dot(acts[:, pl.ds(pl.multiple_of(first, PIECE), PIECE)], cot[cols[k]])

    def grad_to_sib(k, q):
        return remote(gsend.at[k, q], grecv.at[k, q], bg_s, bg_r, k * PIECES + q, dev_s)

    def grad_other(k, q):
        for w in range(2):
            gsend[k, q, w] = grad_block(k, w, other, q).astype(BF16)

    def grad_send(k, q):
        if k == 0:

            @pl.when(c == 0)
            def _():
                if q == 0:
                    load_acts.wait()
                grad_other(k, q)

        else:
            if q == 0:
                remote(cot.at[1 - t], cot.at[1 - t], z_s, z_r, 0, dev_z).wait_recv()
            grad_other(k, q)
        grad_to_sib(k, q).start()

    def grad_keep(k, q):
        grad_to_sib(k, q).wait_recv()
        for w in range(2):
            gsum[k, w, q] = (grad_block(k, w, c, q) + grecv[k, q, w].astype(F32)).astype(BF16)

    def x_send(d):
        return remote(contrib.at[:, lax.rem(x + d, 4)], xr.at[d - 1], xs_s, xs_r, d - 1, dev_x[d - 1])

    def z_send(d):
        return remote(xsum.at[lax.rem(zh + d, 4)], zrecv.at[d - 1], zs_s, zs_r, d - 1, dev_zh[d - 1])

    def z_back(d):
        return remote(frag.at[zh, x], frag.at[zh, x], za_s, za_r, d - 1, dev_zh[d - 1])

    def x_back(d):
        return remote(frag.at[:, x], frag.at[:, x], xa_s, xa_r, d - 1, dev_x[d - 1])

    def outer_own():
        load_mant.wait()
        load_expo.wait()
        power = jnp.exp2(expo[chosen].astype(F32))
        power = jnp.transpose(jnp.concatenate([power] * 4, axis=0))
        for h in range(2):
            block = mant[chosen, :, h * 128 : (h + 1) * 128].astype(F32) * power[:, h : h + 1]
            contrib[:, :, :, h * 128 : (h + 1) * 128] = block.astype(BF16).reshape(4, 4, STATE, 128)
    def outer_1():
        @pl.when(c == 0)
        def _():
            outer_own()

        for d in (1, 2, 3):
            x_send(d).start()

    def outer_2():
        for d in (1, 2, 3):
            x_send(d).wait_recv()
        for i in range(4):
            total = contrib[i, x].astype(F32)
            for d in range(3):
                total = total + xr[d, i].astype(F32)
            xsum[i] = total.astype(BF16)

        @pl.when(c == 1)
        def _():
            pl.semaphore_wait(barrier, len(dev_zh))
            tell(far_sem, dev_s)

        @pl.when(c == 0)
        def _():
            pl.semaphore_wait(far_sem, 1)

        for d in (1, 2, 3):
            z_send(d).start()

    def outer_3():
        load_gw.wait()
        load_mom.wait()
        for d in (1, 2, 3):
            z_send(d).wait_recv()
        total = xsum[zh].astype(F32)
        for d in range(3):
            total = total + zrecv[d].astype(F32)
        delta = total * (1.0 / 16)
        new_moment = BETA * mom[chosen] + delta
        new_weight = gw[chosen] - RATE * (delta + BETA * new_moment)
        for i in range(FRAGS):
            mom_out[i] = jnp.where(chosen == i, new_moment, mom[i])
            gw_out[i] = jnp.where(chosen == i, new_weight, gw[i])
        frag[zh, x] = new_weight.astype(BF16)
        for d in (1, 2, 3):
            z_back(d).start()

    def outer_4():
        for d in (1, 2, 3):
            there = frag.at[lax.rem(zh + 4 - d, 4), x]
            remote(there, there, za_s, za_r, d - 1, dev_zh[d - 1]).wait_recv()
        for d in (1, 2, 3):
            x_back(d).start()

    def outer_5():
        for d in (1, 2, 3):
            there = frag.at[:, lax.rem(x + 4 - d, 4)]
            remote(there, there, xa_s, xa_r, d - 1, dev_x[d - 1]).wait_recv()
        frag_out[...] = frag[...]

    def key_term(w, plane, k):
        wide = pl.ds(pl.multiple_of(column[w] * 2 * ROWS + plane * ROWS, ROWS), ROWS)
        return jnp.dot(acts[:, wide], wbuf[column[w], plane, cols[k]], preferred_element_type=F32)

    def input_block(w, plane):
        for i in range(2):
            rows = pl.ds(i * 512, 512)
            total = nt_dot(cot[0], wbuf[column[w], plane, 0, rows]) + nt_dot(cot[1], wbuf[column[w], plane, 1, rows])
            first = column[w] * 2 * ROWS + plane * ROWS + i * 512
            ig_out[:, pl.ds(pl.multiple_of(first, 512), 512)] = total.astype(BF16)

    def sib_pieces(w, k):
        for q in range(PIECES):
            from_sib(w, k, q).wait_recv()

    send_key = remote(key_send, key_recv, z_s, z_r, 1, dev_z)

    def step(name):
        if name[0] == "G":
            (grad_send if name[1] == "s" else grad_keep)(int(name[2]), int(name[3]))
        elif name[0] == "O":
            (outer_1, outer_2, outer_3, outer_4, outer_5)[int(name[1]) - 1]()
        elif name == "Ka0":
            key[1] = key_term(0, c, 1)
        elif name == "Ka1":
            sib_pieces(0, 1)
            key[1] += key_term(0, other, 1)
        elif name == "Kb":
            key[1] += key_term(1, c, 1)
        elif name == "Kc":
            sib_pieces(1, 1)
            key_send[...] = (key[1] + key_term(1, other, 1)).astype(BF16)
            send_key.start()
        elif name == "Kd0":
            key[0] = key_term(0, c, 0)
            input_block(0, c)
        elif name == "Kd1":
            sib_pieces(0, 0)
            key[0] += key_term(0, other, 0)
            input_block(0, other)
        elif name == "Ke0":
            key[0] += key_term(1, c, 0)
            input_block(1, c)
        elif name == "Ke1":
            sib_pieces(1, 0)
            key[0] += key_term(1, other, 0)
            input_block(1, other)
        else:
            send_key.wait_recv()
            key_out[...] = (key[0] + key_recv[...].astype(F32)).astype(BF16)

    own_pieces = {"Ka0": (0, 1), "Kb": (1, 1), "Kd0": (0, 0), "Ke0": (1, 0)}

    load_cot.wait()

    @pl.when(c == 0)
    def _():
        pl.semaphore_wait(barrier, 4 + len(dev_x))
        tell(group_sem, dev_h, dev_v, dev_z, *dev_x)

    @pl.when(c == 1)
    def _():
        load_acts.wait()
        for q in range(PIECES):
            grad_other(0, q)
        outer_own()
        pl.semaphore_wait(go_sem, 1)
        tell(barrier, *dev_zh)

    for i, name in enumerate((*STEPS, None)):
        if i == 1:

            @pl.when(c == 0)
            def _():
                pl.semaphore_wait(group_sem, 3 + len(dev_x))
                tell(go_sem, dev_s)

        for here, role, plan in roles:

            @pl.when(here)
            def _(role=role, tasks=plan[i], name=name):
                for task in tasks:
                    role.do(*task)
                if name in own_pieces:
                    for q in range(PIECES):
                        role.have(*own_pieces[name], q)

        if name is not None:
            step(name)

    send_key.wait_send()
    for d in (1, 2, 3):
        for copy in (x_send(d), z_send(d), z_back(d), x_back(d)):
            copy.wait_send()
    for k in range(2):
        for q in range(PIECES):
            grad_to_sib(k, q).wait_send()
    for here, role, plan in roles:

        @pl.when(here)
        def _(role=role, plan=plan):
            for tasks in plan:
                for task in tasks:
                    if role.sent(*task):
                        role.copy(*task).wait_send()


def deliver(*refs):
    sem = refs[-1]
    half = len(refs) // 2
    pairs = list(zip(refs[:half], refs[half:-1]))
    ig, ig_out = pairs.pop(1)
    quarter = TOK // 4
    for n in range(4):
        rows = pl.ds(n * quarter, quarter)
        pairs.append((ig.at[rows], ig_out.at[rows]))
    copies = [pltpu.make_async_copy(a, b, sem.at[i]) for i, (a, b) in enumerate(pairs)]
    for copy in copies:
        copy.start()
    for copy in copies:
        copy.wait()


def local(
    activations, key_weight, key_cotangent, outer_mantissa, outer_exponent, round_index, global_weight, outer_momentum
):
    vmem = pltpu.VMEM
    dma = lambda n: pltpu.SemaphoreType.DMA((n,))
    hold = lambda v: pltpu.with_memory_space_constraint(v, pltpu.HBM)
    exponent = jnp.transpose(outer_exponent[0], (0, 2, 1))
    anywhere = pl.BlockSpec(memory_space=pl.ANY)
    near_by = pl.BlockSpec(memory_space=pltpu.VMEM)
    n = PIECES
    outs = pl.pallas_call(
        kernel,
        out_shape=(
            jax.ShapeDtypeStruct((TOK, COLS), BF16),
            jax.ShapeDtypeStruct((TOK, WIDTH), BF16),
            jax.ShapeDtypeStruct((n, PIECE, COLS), BF16),
            jax.ShapeDtypeStruct((FRAGS, STATE, COLS), F32),
            jax.ShapeDtypeStruct((FRAGS, STATE, COLS), F32),
            jax.ShapeDtypeStruct((4, 4, STATE, COLS), BF16),
        ),
        in_specs=[anywhere] * 5 + [pl.BlockSpec(memory_space=pltpu.SMEM)] + [anywhere] * 2,
        out_specs=[near_by] * 6,
        scratch_shapes=[
            vmem((TOK, WIDTH), BF16),
            vmem((2, TOK, COLS), BF16),
            vmem((2, 2, 2, ROWS, COLS), BF16),
            vmem((2, n, 2, PIECE, COLS), BF16),
            vmem((2, n, 2, PIECE, COLS), BF16),
            vmem((2, 2, n, PIECE, COLS), BF16),
            vmem((2, 2, n, PIECE, COLS), BF16),
            vmem((2, n, PIECE, COLS), BF16),
            vmem((n, PIECE, COLS), BF16),
            vmem((2, TOK, COLS), F32),
            vmem((TOK, COLS), BF16),
            vmem((TOK, COLS), BF16),
            vmem((FRAGS, ROWS, COLS), BF16),
            vmem((FRAGS, 2, ROWS), jnp.int32),
            vmem((4, 4, STATE, COLS), BF16),
            vmem((3, 4, STATE, COLS), BF16),
            vmem((4, STATE, COLS), BF16),
            vmem((3, STATE, COLS), BF16),
            vmem((4, 4, STATE, COLS), BF16),
            vmem((FRAGS, STATE, COLS), F32),
            vmem((FRAGS, STATE, COLS), F32),
            dma(len(LOADS)),
            dma(4 * n), dma(4 * n), dma(2 * n), dma(2 * n), dma(4 * n), dma(4 * n), dma(2 * n), dma(2 * n),
            dma(4 * n), dma(4 * n), dma(2 * n), dma(2 * n), dma(2 + 2 * n), dma(2 + 2 * n),
            dma(3), dma(3), dma(3), dma(3), dma(3), dma(3), dma(3), dma(3),
            pltpu.SemaphoreType.REGULAR, pltpu.SemaphoreType.REGULAR, pltpu.SemaphoreType.REGULAR,
        ],
        compiler_params=pltpu.CompilerParams(
            collective_id=0, has_side_effects=True, vmem_limit_bytes=44 * 2**20
        ),
    )(
        hold(activations), hold(key_weight[0]), hold(key_cotangent), hold(outer_mantissa[0]), hold(exponent),
        round_index, hold(global_weight), hold(outer_momentum),
    )
    outs = pl.pallas_call(
        deliver,
        out_shape=tuple(jax.ShapeDtypeStruct(o.shape, o.dtype) for o in outs),
        in_specs=[anywhere] * 6,
        out_specs=[anywhere] * 6,
        scratch_shapes=[dma(9)],
        compiler_params=pltpu.CompilerParams(vmem_limit_bytes=2**20),
    )(*outs)
    key_states, input_grad, weight_grad, global_weight_out, momentum_out, fragment_weight = outs
    return (
        key_states,
        input_grad,
        weight_grad.reshape(1, ROWS, COLS),
        global_weight_out,
        momentum_out,
        fragment_weight.reshape(ROWS, COLS),
    )


def solution(mesh):
    placed = (
        P(("replica", "fsdp"), "tensor"),
        P("replica", "fsdp", "tensor"),
        P(("replica", "fsdp"), "tensor"),
        P("replica", None, "fsdp", "tensor"),
        P("replica", None, "fsdp", "tensor"),
        P(),
        P(None, ("fsdp", "replica"), "tensor"),
        P(None, ("fsdp", "replica"), "tensor"),
    )
    return jax.shard_map(
        local,
        mesh=mesh,
        in_specs=placed,
        out_specs=(
            P(("replica", "fsdp"), "tensor"),
            P(("replica", "fsdp"), "tensor"),
            P("replica", "fsdp", "tensor"),
            P(None, ("fsdp", "replica"), "tensor"),
            P(None, ("fsdp", "replica"), "tensor"),
            P("fsdp", "tensor"),
        ),
        check_vma=False,
    )
```

```python
import jax
import jax.numpy as jnp
from jax import lax
from jax.experimental import pallas as pl
from jax.experimental.pallas import tpu as pltpu
from jax.sharding import PartitionSpec as P

MESH = pl.DeviceIdType.MESH
F32 = jnp.float32
BF16 = jnp.bfloat16

TOK = 384
ROWS = 1024
COLS = 256
WIDTH = 4096
STATE = 64
FRAGS = 4
RATE = 0.7
BETA = 0.9
PIECES = 4
PIECE = ROWS // PIECES
WEIGHT_ROUTE = ((4, 2, 2, 1), (2, 1, 2, 4))
GRAD_ROUTE = ((2, 1, 4, 2), (2, 4, 1, 2))
LOADS = ("cot", "weight", "acts", "mant", "expo", "gw", "mom")

STEPS = (
    "Gs00", "Gs01", "Gs02", "Gs03", "O1", "Gk00", "Gk01", "Gk02", "Gk03",
    "Gs10", "Gs11", "Gs12", "Gs13", "Gk10", "Gk11", "Gk12", "Gk13", "O2", "O3", "Ka0",
    "Ka1", "Kb", "Kc", "O4", "Kd0", "Kd1", "Ke0", "Ke1", "O5", "Kf",
)
NEAR = (
    (
        ("cot", 0, 0, 0), ("s", 0, 0, 3), ("v", 0, 0, 2), ("h", 0, 0, 1), ("s", 0, 0, 2), ("s", 0, 0, 0),
    ),
    (),
    (),
    (),
    (),
    (),
    (
        ("gh", 1, 0, 0), ("v", 0, 0, 3),
    ),
    (
        ("s", 0, 0, 1),
    ),
    (),
    (
        ("s", 1, 0, 1), ("gv", 1, 0, 2), ("h", 0, 0, 2),
    ),
    (),
    (),
    (),
    (),
    (),
    (
        ("gv", 1, 1, 1), ("s", 0, 1, 3),
    ),
    (
        ("gh", 1, 1, 0),
    ),
    (
        ("s", 1, 0, 2),
    ),
    (
        ("v", 0, 1, 3), ("s", 0, 1, 2), ("gh", 1, 0, 1), ("v", 0, 0, 0), ("gh", 1, 1, 2), ("s", 0, 1, 0),
        ("f", 0, 0, 1), ("v", 0, 1, 0), ("h", 0, 1, 2), ("f", 0, 1, 2), ("s", 0, 1, 1), ("h", 0, 1, 1),
        ("v", 0, 1, 2), ("f", 0, 1, 0), ("s", 1, 1, 2), ("f", 0, 0, 0), ("v", 0, 1, 1), ("h", 0, 1, 0),
    ),
    (),
    (),
    (
        ("s", 1, 1, 1), ("v", 1, 1, 1), ("h", 0, 0, 3), ("f", 0, 1, 1), ("s", 1, 1, 0), ("s", 1, 1, 3),
    ),
    (
        ("gh", 1, 0, 3), ("v", 0, 0, 1),
    ),
    (
        ("s", 1, 0, 3), ("s", 1, 0, 0), ("v", 1, 0, 3), ("gh", 1, 1, 3),
    ),
    (),
    (),
    (),
    (),
    (
        ("f", 0, 0, 3), ("f", 0, 1, 3), ("f", 0, 0, 2),
    ),
    (),
    (),
)
FAR = (
    (
        ("cot", 0, 0, 0),
    ),
    (),
    (),
    (),
    (),
    (),
    (
        ("gh", 1, 0, 0),
    ),
    (
        ("gv", 0, 0, 1),
    ),
    (
        ("z", 0, 1, 3),
    ),
    (
        ("s", 0, 0, 2), ("h", 0, 0, 2),
    ),
    (),
    (),
    (),
    (
        ("gv", 1, 0, 1), ("z", 0, 1, 2), ("s", 0, 0, 3),
    ),
    (),
    (
        ("gh", 1, 1, 0),
    ),
    (
        ("gv", 1, 1, 2),
    ),
    (
        ("z", 0, 1, 0), ("s", 1, 0, 2), ("gh", 1, 1, 3),
    ),
    (
        ("gv", 0, 1, 2), ("gh", 1, 1, 1), ("gv", 0, 1, 0), ("z", 0, 1, 1), ("s", 0, 1, 3), ("h", 0, 1, 3),
        ("gv", 0, 0, 0), ("s", 0, 0, 0), ("h", 0, 0, 0), ("gv", 0, 1, 1), ("s", 1, 1, 3), ("s", 0, 1, 0),
        ("h", 0, 1, 0),
    ),
    (
        ("v", 1, 1, 3), ("f", 0, 1, 2), ("s", 1, 0, 0), ("s", 0, 1, 2), ("h", 0, 1, 2), ("v", 1, 0, 0),
        ("f", 0, 1, 0), ("s", 1, 1, 0),
    ),
    (
        ("s", 0, 1, 1), ("gh", 1, 0, 3), ("gv", 0, 1, 3),
    ),
    (
        ("s", 1, 1, 2),
    ),
    (
        ("s", 1, 1, 1), ("gh", 1, 0, 2), ("f", 0, 1, 1),
    ),
    (
        ("gv", 0, 0, 3), ("s", 0, 0, 1), ("h", 0, 0, 1),
    ),
    (),
    (),
    (
        ("gv", 0, 0, 2), ("s", 1, 0, 3),
    ),
    (
        ("s", 1, 0, 1),
    ),
    (
        ("f", 0, 1, 3),
    ),
    (),
    (),
)


def tt_dot(a, b):
    return lax.dot_general(a, b, (((0,), (0,)), ((), ())), preferred_element_type=F32)


def nt_dot(a, b):
    return lax.dot_general(a, b, (((1,), (1,)), ((), ())), preferred_element_type=F32)


def kernel(
    acts_hbm, weight_hbm, cot_hbm, mant_hbm, expo_hbm, round_ref, gw_hbm, mom_hbm,
    key_out, ig_out, wg_out, gw_out, mom_out, frag_out,
    acts, cot, wbuf, gsend, grecv, gsum, rv, rh, zr, key, key_send, key_recv,
    mant, expo, contrib, xr, xsum, zrecv, frag, gw, mom,
    ld, wv_s, wv_r, wh_s, wh_r, rv_s, rv_r, rh_s, rh_r, bw_s, bw_r, bg_s, bg_r, z_s, z_r,
    xs_s, xs_r, zs_s, zs_r, za_s, za_r, xa_s, xa_r, group_sem, go_sem, far_sem,
):
    r = lax.axis_index("replica")
    f = lax.axis_index("fsdp")
    t = lax.axis_index("tensor")
    zh, x = r // 4, lax.rem(r, 4)
    y, c = f // 2, lax.rem(f, 2)
    odd = lax.rem(y, 2)
    near = (y // 2) == t
    far = (y // 2) != t
    ja = jnp.where(near, odd, 1 - odd)
    column = (ja, 1 - ja)
    cols = (t, 1 - t)
    dev_h = (r, (y + 1 - 2 * odd) * 2 + c, t)
    dev_v = (r, (3 - y) * 2 + c, t)
    dev_z = (r, f, 1 - t)
    dev_s = (r, y * 2 + 1 - c, t)
    dev_x = [(zh * 4 + lax.rem(x + d, 4), f, t) for d in (1, 2, 3)]
    dev_zh = [(lax.rem(zh + d, 4) * 4 + x, f, t) for d in (1, 2, 3)]

    barrier = pltpu.get_barrier_semaphore()

    def tell(sem, *devices):
        for device in devices:
            pl.semaphore_signal(sem, inc=1, device_id=device, device_id_type=MESH)

    @pl.when(c == 0)
    def _():
        tell(barrier, dev_h, dev_v, dev_z, *dev_x)

    @pl.when(c == 1)
    def _():
        tell(barrier, dev_s)

    def load(name, src, dst):
        return pltpu.make_async_copy(src, dst, ld.at[LOADS.index(name)])

    def remote(src, dst, s, r_, i, device):
        return pltpu.make_async_remote_copy(
            src_ref=src, dst_ref=dst, send_sem=s.at[i], recv_sem=r_.at[i], device_id=device, device_id_type=MESH
        )

    load_cot = load("cot", cot_hbm, cot.at[t])
    load_weight = load("weight", weight_hbm, wbuf.at[ja, c, t])
    load_acts = load("acts", acts_hbm, acts)
    load_mant = load("mant", mant_hbm, mant)
    load_expo = load("expo", expo_hbm, expo)
    load_gw = load("gw", gw_hbm, gw)
    load_mom = load("mom", mom_hbm, mom)
    load_cot.start()

    @pl.when(near)
    def _():
        load_weight.start()

    for one in (load_acts, load_mant, load_expo, load_gw, load_mom):
        one.start()

    def piece(w, plane, k, q):
        return wbuf.at[column[w], plane, cols[k], pl.ds(q * PIECE, PIECE)]

    def at(w, k, q):
        return (w * 2 + k) * PIECES + q

    def part(w, k, q):
        return gsum.at[k, w, q]

    def from_sib(w, k, q):
        there = piece(w, 1 - c, k, q)
        return remote(there, there, bw_s, bw_r, at(w, k, q), dev_s)

    def copy_of(name, w, k, q):
        if name == "v":
            return remote(piece(w, c, k, q), piece(w, c, k, q), wv_s, wv_r, at(w, k, q), dev_v)
        if name == "h":
            return remote(piece(w, c, k, q), piece(w, c, k, q), wh_s, wh_r, at(0, k, q), dev_h)
        if name == "s":
            return remote(piece(w, c, k, q), piece(w, c, k, q), bw_s, bw_r, at(w, k, q), dev_s)
        if name == "z":
            rows = pl.ds(q * PIECE, PIECE)
            return remote(weight_hbm.at[rows], wbuf.at[odd, c, t, rows], z_s, z_r, 2 + q, dev_z)
        if name == "gv":
            src = part(w, k, q)
            if w == 0 and GRAD_ROUTE[k][q] != 1:
                src = rh.at[k, q]
            return remote(src, rv.at[w, k, q], rv_s, rv_r, at(w, k, q), dev_v)
        if name == "f":
            return remote(rv.at[0, k, q], zr.at[q], z_s, z_r, 2 + PIECES + q, dev_z)
        return remote(cot.at[t], cot.at[t], z_s, z_r, 0, dev_z)

    def grad_h(is_near, k, q):
        route = GRAD_ROUTE[k][q]
        src = rv.at[1, k, q] if route == (1 if is_near else 4) else part(1, k, q)
        return remote(src, rh.at[k, q], rh_s, rh_r, at(0, k, q), dev_h)

    def add_into(dst, *others):
        total = dst[...].astype(F32)
        for other in others:
            total = total + other[...].astype(F32)
        dst[...] = total.astype(BF16)

    class Role:
        def __init__(self, is_near):
            self.is_near = is_near
            self.seen = set()

        def once(self, key, *copy):
            if key not in self.seen:
                self.seen.add(key)
                remote(*copy).wait_recv()

        def have(self, w, k, q):
            there = piece(w, c, k, q)
            if self.is_near and w == 0:
                if k == 0:
                    if "weight" not in self.seen:
                        self.seen.add("weight")
                        load_weight.wait()
                else:
                    self.once(("z", q), there, there, z_s, z_r, 2 + q, dev_z)
                return
            over_v = (WEIGHT_ROUTE[k][q] == 4) if self.is_near else (w == 0 or WEIGHT_ROUTE[k][q] == 1)
            if over_v:
                self.once(("v", w, k, q), there, there, wv_s, wv_r, at(w, k, q), dev_v)
            else:
                self.once(("h", w, k, q), there, there, wh_s, wh_r, at(0, k, q), dev_h)

        def have_v(self, w, k, q):
            there = rv.at[w, k, q]
            self.once(("gv", w, k, q), there, there, rv_s, rv_r, at(w, k, q), dev_v)

        def have_h(self, k, q):
            there = rh.at[k, q]
            self.once(("gh", k, q), there, there, rh_s, rh_r, at(0, k, q), dev_h)

        def copy(self, name, w, k, q):
            return grad_h(self.is_near, k, q) if name == "gh" else copy_of(name, w, k, q)

        def do(self, name, w, k, q):
            if name in ("v", "h", "s"):
                self.have(w, k, q)
            elif name == "cot":
                pass
            elif name == "gh":
                if GRAD_ROUTE[k][q] == (1 if self.is_near else 4):
                    self.have_v(1, k, q)
                    add_into(rv.at[1, k, q], part(1, k, q))
            elif name == "gv":
                if w == 0 and GRAD_ROUTE[k][q] != 1:
                    self.have_h(k, q)
                    add_into(rh.at[k, q], part(0, k, q))
            elif name == "f":
                if not self.is_near:
                    remote(zr.at[q], zr.at[q], z_s, z_r, 2 + PIECES + q, dev_z).wait_recv()
                    wg_out[q] = zr[q]
                    return
                self.have_v(0, k, q)
                terms = [part(0, k, q)]
                if GRAD_ROUTE[k][q] != 4:
                    self.have_h(k, q)
                    terms.append(rh.at[k, q])
                add_into(rv.at[0, k, q], *terms)
                if k == 0:
                    wg_out[q] = rv[0, k, q]
                    return
            self.copy(name, w, k, q).start()

        def sent(self, name, w, k, q):
            return not (name == "f" and (k == 0 or not self.is_near))

    roles = ((near, Role(True), NEAR), (far, Role(False), FAR))
    chosen = lax.rem(round_ref[0], FRAGS)
    other = 1 - c

    def grad_block(k, w, plane, q):
        first = column[w] * 2 * ROWS + plane * ROWS + q * PIECE
        return tt_dot(acts[:, pl.ds(pl.multiple_of(first, PIECE), PIECE)], cot[cols[k]])

    def grad_to_sib(k, q):
        return remote(gsend.at[k, q], grecv.at[k, q], bg_s, bg_r, k * PIECES + q, dev_s)

    def grad_other(k, q):
        for w in range(2):
            gsend[k, q, w] = grad_block(k, w, other, q).astype(BF16)

    def grad_send(k, q):
        if k == 0:

            @pl.when(c == 0)
            def _():
                if q == 0:
                    load_acts.wait()
                grad_other(k, q)

        else:
            if q == 0:
                remote(cot.at[1 - t], cot.at[1 - t], z_s, z_r, 0, dev_z).wait_recv()
            grad_other(k, q)
        grad_to_sib(k, q).start()

    def grad_keep(k, q):
        grad_to_sib(k, q).wait_recv()
        for w in range(2):
            gsum[k, w, q] = (grad_block(k, w, c, q) + grecv[k, q, w].astype(F32)).astype(BF16)

    def x_send(d):
        return remote(contrib.at[:, lax.rem(x + d, 4)], xr.at[d - 1], xs_s, xs_r, d - 1, dev_x[d - 1])

    def z_send(d):
        return remote(xsum.at[lax.rem(zh + d, 4)], zrecv.at[d - 1], zs_s, zs_r, d - 1, dev_zh[d - 1])

    def z_back(d):
        return remote(frag.at[zh, x], frag.at[zh, x], za_s, za_r, d - 1, dev_zh[d - 1])

    def x_back(d):
        return remote(frag.at[:, x], frag.at[:, x], xa_s, xa_r, d - 1, dev_x[d - 1])

    def outer_own():
        load_mant.wait()
        load_expo.wait()
        power = jnp.exp2(expo[chosen].astype(F32))
        power = jnp.transpose(jnp.concatenate([power] * 4, axis=0))
        for h in range(2):
            block = mant[chosen, :, h * 128 : (h + 1) * 128].astype(F32) * power[:, h : h + 1]
            contrib[:, :, :, h * 128 : (h + 1) * 128] = block.astype(BF16).reshape(4, 4, STATE, 128)
    def outer_1():
        @pl.when(c == 0)
        def _():
            outer_own()

        for d in (1, 2, 3):
            x_send(d).start()

    def outer_2():
        for d in (1, 2, 3):
            x_send(d).wait_recv()
        for i in range(4):
            total = contrib[i, x].astype(F32)
            for d in range(3):
                total = total + xr[d, i].astype(F32)
            xsum[i] = total.astype(BF16)

        @pl.when(c == 1)
        def _():
            pl.semaphore_wait(barrier, len(dev_zh))
            tell(far_sem, dev_s)

        @pl.when(c == 0)
        def _():
            pl.semaphore_wait(far_sem, 1)

        for d in (1, 2, 3):
            z_send(d).start()

    def outer_3():
        load_gw.wait()
        load_mom.wait()
        for d in (1, 2, 3):
            z_send(d).wait_recv()
        total = xsum[zh].astype(F32)
        for d in range(3):
            total = total + zrecv[d].astype(F32)
        delta = total * (1.0 / 16)
        new_moment = BETA * mom[chosen] + delta
        new_weight = gw[chosen] - RATE * (delta + BETA * new_moment)
        for i in range(FRAGS):
            mom_out[i] = jnp.where(chosen == i, new_moment, mom[i])
            gw_out[i] = jnp.where(chosen == i, new_weight, gw[i])
        frag[zh, x] = new_weight.astype(BF16)
        for d in (1, 2, 3):
            z_back(d).start()

    def outer_4():
        for d in (1, 2, 3):
            there = frag.at[lax.rem(zh + 4 - d, 4), x]
            remote(there, there, za_s, za_r, d - 1, dev_zh[d - 1]).wait_recv()
        for d in (1, 2, 3):
            x_back(d).start()

    def outer_5():
        for d in (1, 2, 3):
            there = frag.at[:, lax.rem(x + 4 - d, 4)]
            remote(there, there, xa_s, xa_r, d - 1, dev_x[d - 1]).wait_recv()
        frag_out[...] = frag[...]

    def key_term(w, plane, k):
        wide = pl.ds(pl.multiple_of(column[w] * 2 * ROWS + plane * ROWS, ROWS), ROWS)
        return jnp.dot(acts[:, wide], wbuf[column[w], plane, cols[k]], preferred_element_type=F32)

    def input_block(w, plane):
        for i in range(2):
            rows = pl.ds(i * 512, 512)
            total = nt_dot(cot[0], wbuf[column[w], plane, 0, rows]) + nt_dot(cot[1], wbuf[column[w], plane, 1, rows])
            first = column[w] * 2 * ROWS + plane * ROWS + i * 512
            ig_out[:, pl.ds(pl.multiple_of(first, 512), 512)] = total.astype(BF16)

    def sib_pieces(w, k):
        for q in range(PIECES):
            from_sib(w, k, q).wait_recv()

    send_key = remote(key_send, key_recv, z_s, z_r, 1, dev_z)

    def step(name):
        if name[0] == "G":
            (grad_send if name[1] == "s" else grad_keep)(int(name[2]), int(name[3]))
        elif name[0] == "O":
            (outer_1, outer_2, outer_3, outer_4, outer_5)[int(name[1]) - 1]()
        elif name == "Ka0":
            key[1] = key_term(0, c, 1)
        elif name == "Ka1":
            sib_pieces(0, 1)
            key[1] += key_term(0, other, 1)
        elif name == "Kb":
            key[1] += key_term(1, c, 1)
        elif name == "Kc":
            sib_pieces(1, 1)
            key_send[...] = (key[1] + key_term(1, other, 1)).astype(BF16)
            send_key.start()
        elif name == "Kd0":
            key[0] = key_term(0, c, 0)
            input_block(0, c)
        elif name == "Kd1":
            sib_pieces(0, 0)
            key[0] += key_term(0, other, 0)
            input_block(0, other)
        elif name == "Ke0":
            key[0] += key_term(1, c, 0)
            input_block(1, c)
        elif name == "Ke1":
            sib_pieces(1, 0)
            key[0] += key_term(1, other, 0)
            input_block(1, other)
        else:
            send_key.wait_recv()
            key_out[...] = (key[0] + key_recv[...].astype(F32)).astype(BF16)

    own_pieces = {"Ka0": (0, 1), "Kb": (1, 1), "Kd0": (0, 0), "Ke0": (1, 0)}

    load_cot.wait()

    @pl.when(c == 0)
    def _():
        pl.semaphore_wait(barrier, 4 + len(dev_x))
        tell(group_sem, dev_h, dev_v, dev_z, *dev_x)

    @pl.when(c == 1)
    def _():
        load_acts.wait()
        for q in range(PIECES):
            grad_other(0, q)
        outer_own()
        pl.semaphore_wait(go_sem, 1)
        tell(barrier, *dev_zh)

    for i, name in enumerate((*STEPS, None)):
        if i == 1:

            @pl.when(c == 0)
            def _():
                pl.semaphore_wait(group_sem, 3 + len(dev_x))
                tell(go_sem, dev_s)

        for here, role, plan in roles:

            @pl.when(here)
            def _(role=role, tasks=plan[i], name=name):
                for task in tasks:
                    role.do(*task)
                if name in own_pieces:
                    for q in range(PIECES):
                        role.have(*own_pieces[name], q)

        if name is not None:
            step(name)

    send_key.wait_send()
    for d in (1, 2, 3):
        for copy in (x_send(d), z_send(d), z_back(d), x_back(d)):
            copy.wait_send()
    for k in range(2):
        for q in range(PIECES):
            grad_to_sib(k, q).wait_send()
    for here, role, plan in roles:

        @pl.when(here)
        def _(role=role, plan=plan):
            for tasks in plan:
                for task in tasks:
                    if role.sent(*task):
                        role.copy(*task).wait_send()


def deliver(*refs):
    sem = refs[-1]
    half = len(refs) // 2
    small = list(zip(refs[:half], refs[half:-1]))
    ig, ig_out = small.pop(1)
    quarter = TOK // 4
    pairs = []
    for n in range(4):
        rows = pl.ds(n * quarter, quarter)
        pairs.append((ig.at[rows], ig_out.at[rows]))
    pairs += small
    copies = [pltpu.make_async_copy(a, b, sem.at[i]) for i, (a, b) in enumerate(pairs)]
    for copy in copies:
        copy.start()
    for copy in copies:
        copy.wait()


def local(
    activations, key_weight, key_cotangent, outer_mantissa, outer_exponent, round_index, global_weight, outer_momentum
):
    vmem = pltpu.VMEM
    dma = lambda n: pltpu.SemaphoreType.DMA((n,))
    hold = lambda v: pltpu.with_memory_space_constraint(v, pltpu.HBM)
    exponent = jnp.transpose(outer_exponent[0], (0, 2, 1))
    anywhere = pl.BlockSpec(memory_space=pl.ANY)
    near_by = pl.BlockSpec(memory_space=pltpu.VMEM)
    n = PIECES
    outs = pl.pallas_call(
        kernel,
        out_shape=(
            jax.ShapeDtypeStruct((TOK, COLS), BF16),
            jax.ShapeDtypeStruct((TOK, WIDTH), BF16),
            jax.ShapeDtypeStruct((n, PIECE, COLS), BF16),
            jax.ShapeDtypeStruct((FRAGS, STATE, COLS), F32),
            jax.ShapeDtypeStruct((FRAGS, STATE, COLS), F32),
            jax.ShapeDtypeStruct((4, 4, STATE, COLS), BF16),
        ),
        in_specs=[anywhere] * 5 + [pl.BlockSpec(memory_space=pltpu.SMEM)] + [anywhere] * 2,
        out_specs=[near_by] * 6,
        scratch_shapes=[
            vmem((TOK, WIDTH), BF16),
            vmem((2, TOK, COLS), BF16),
            vmem((2, 2, 2, ROWS, COLS), BF16),
            vmem((2, n, 2, PIECE, COLS), BF16),
            vmem((2, n, 2, PIECE, COLS), BF16),
            vmem((2, 2, n, PIECE, COLS), BF16),
            vmem((2, 2, n, PIECE, COLS), BF16),
            vmem((2, n, PIECE, COLS), BF16),
            vmem((n, PIECE, COLS), BF16),
            vmem((2, TOK, COLS), F32),
            vmem((TOK, COLS), BF16),
            vmem((TOK, COLS), BF16),
            vmem((FRAGS, ROWS, COLS), BF16),
            vmem((FRAGS, 2, ROWS), jnp.int32),
            vmem((4, 4, STATE, COLS), BF16),
            vmem((3, 4, STATE, COLS), BF16),
            vmem((4, STATE, COLS), BF16),
            vmem((3, STATE, COLS), BF16),
            vmem((4, 4, STATE, COLS), BF16),
            vmem((FRAGS, STATE, COLS), F32),
            vmem((FRAGS, STATE, COLS), F32),
            dma(len(LOADS)),
            dma(4 * n), dma(4 * n), dma(2 * n), dma(2 * n), dma(4 * n), dma(4 * n), dma(2 * n), dma(2 * n),
            dma(4 * n), dma(4 * n), dma(2 * n), dma(2 * n), dma(2 + 2 * n), dma(2 + 2 * n),
            dma(3), dma(3), dma(3), dma(3), dma(3), dma(3), dma(3), dma(3),
            pltpu.SemaphoreType.REGULAR, pltpu.SemaphoreType.REGULAR, pltpu.SemaphoreType.REGULAR,
        ],
        compiler_params=pltpu.CompilerParams(
            collective_id=0, has_side_effects=True, vmem_limit_bytes=44 * 2**20
        ),
    )(
        hold(activations), hold(key_weight[0]), hold(key_cotangent), hold(outer_mantissa[0]), hold(exponent),
        round_index, hold(global_weight), hold(outer_momentum),
    )
    outs = pl.pallas_call(
        deliver,
        out_shape=tuple(jax.ShapeDtypeStruct(o.shape, o.dtype) for o in outs),
        in_specs=[anywhere] * 6,
        out_specs=[anywhere] * 6,
        scratch_shapes=[dma(9)],
        compiler_params=pltpu.CompilerParams(vmem_limit_bytes=2**20),
    )(*outs)
    key_states, input_grad, weight_grad, global_weight_out, momentum_out, fragment_weight = outs
    return (
        key_states,
        input_grad,
        weight_grad.reshape(1, ROWS, COLS),
        global_weight_out,
        momentum_out,
        fragment_weight.reshape(ROWS, COLS),
    )


def solution(mesh):
    placed = (
        P(("replica", "fsdp"), "tensor"),
        P("replica", "fsdp", "tensor"),
        P(("replica", "fsdp"), "tensor"),
        P("replica", None, "fsdp", "tensor"),
        P("replica", None, "fsdp", "tensor"),
        P(),
        P(None, ("fsdp", "replica"), "tensor"),
        P(None, ("fsdp", "replica"), "tensor"),
    )
    return jax.shard_map(
        local,
        mesh=mesh,
        in_specs=placed,
        out_specs=(
            P(("replica", "fsdp"), "tensor"),
            P(("replica", "fsdp"), "tensor"),
            P("replica", "fsdp", "tensor"),
            P(None, ("fsdp", "replica"), "tensor"),
            P(None, ("fsdp", "replica"), "tensor"),
            P("fsdp", "tensor"),
        ),
        check_vma=False,
    )
```
